128 devices in a mesh: row: 32 (over z, y, core), col: 4 (over x).
Axes of the slice: x: 4, y: 4, z: 4, core: 2. Of those that a mesh axis runs over, the one named last changes fastest.
Arguments:
- features: float32 [131072, 128], P('row'), may hold values from -6 to 6
- inv_length: float32 [128], replicated, may hold values from 0.03 to 0.3
- nugget: float32 [131072], P('row'), may hold values from 0.5 to 1.5
- pairs: int32 [2, 131072], replicated, may hold values from 0 to 131071, as said below
- weights: float32 [131072], replicated, may hold values from 0.2 to 2
Outputs:
- factor: float32 [2, 131072, 512], P(None, 'row', 'col')
- schur: float32 [131072, 512], P('row', 'col')
The draws below stay inside these ranges and needn't reach their ends.
Inputs may be any that keep to these rules, and one draw needn't show every extreme that they name: `pairs`: every configuration is the winner of exactly one pair; a pair's loser minus its winner, modulo 131072, lies in 1 to 1023.
All inputs are finite; a program needn't handle non-finite values.
Results may differ from the reference program's by a relative error of at most 0.0003.
Values sent between devices are 32-bit elements; how exact they have to be, the bound alone decides.
No kernel may reach another device: no remote copies, remote signals or barrier semaphores. Data moves between devices by JAX's collectives and lax.ppermute only.
A program may use at most 192 MiB of HBM per device.

```python
import math
import jax
import jax.numpy as jnp
from jax import lax

F = 128
PANEL = 512
SPAN = 1024
ROWS_DEV = 4096
CONFIGS = 131072


def draw_pairs(key, part):
    key = jax.random.fold_in(key, 7)
    first_key, second_key = jax.random.split(key)
    winner = jax.random.permutation(first_key, CONFIGS).astype(jnp.int32)
    offset = jax.random.randint(second_key, (CONFIGS,), 1, SPAN, dtype=jnp.int32)
    losing = (winner + offset) % CONFIGS
    return jnp.stack([winner, losing]).astype(jnp.int32)


def block_levels(own_key, extent, cuts, low, top_value):
    factor_of = 1.0
    for position, parts in cuts:
        heights = jax.random.uniform(jax.random.fold_in(jax.random.fold_in(own_key, 6), position), (parts,), jnp.float32, low / len(cuts), top_value / len(cuts))
        factor_of = factor_of * jnp.repeat(jnp.exp(heights), extent[position] // parts).reshape((-1,) + (1,) * (len(extent) - 1 - position))
    return factor_of


def normal_values(rng, shape, width, bound, cuts=(), kind=jnp.bfloat16):
    entries = width * jax.random.normal(rng, shape, jnp.float32)
    if cuts:
        entries = entries * block_levels(rng, shape, cuts, -0.22, 0.18)
    return jnp.clip(entries, -bound, bound).astype(kind)


def setup_inputs(seed: int = 0) -> dict:
    key_list = jax.random.split(jax.random.key(seed), 6)
    return {
        "features": normal_values(key_list[0], (CONFIGS, F), 1.0, 6.0, ((0, 32),), jnp.float32),
        "inv_length": jnp.clip(jnp.exp(jax.random.uniform(key_list[1], (F,), jnp.float32, math.log(0.03), math.log(0.3))), 0.03, 0.3),
        "nugget": jnp.clip(0.5 + 1.0 * jax.random.uniform(key_list[2], (CONFIGS,), jnp.float32) ** block_levels(key_list[2], (CONFIGS,), ((0, 32),), -0.2, 0.2), 0.5, 1.5),
        "pairs": draw_pairs(jax.random.fold_in(key_list[5], 71), 0),
        "weights": jnp.clip(jnp.exp(jax.random.uniform(key_list[4], (CONFIGS,), jnp.float32, math.log(0.2), math.log(2.0))), 0.2, 2.0),
    }


signal_variance = 2.0

def column_slots(glob_ids, base_col, span_rows, narrow):
    slots = jnp.full(glob_ids.shape, 3 * narrow, jnp.int32)
    for target in range(3):
        offset = glob_ids - target * span_rows - base_col
        slots = jnp.where((offset >= 0) & (offset < narrow), target * narrow + offset, slots)
    return slots.astype(jnp.int32)

def kernel_block(scaled, columns):
    own_sq = jnp.sum(scaled * scaled, axis=1)
    col_sq = jnp.sum(columns * columns, axis=1)
    inner = jnp.einsum('if,jf->ij', scaled, columns, precision=lax.Precision.HIGHEST)
    distance = own_sq[:, None] + col_sq[None, :] - 2.0 * inner
    return signal_variance * jnp.exp(-0.5 * distance)

def reference(features, inv_length, nugget, pairs, weights):
    configs = features.shape[0]
    scaled = features * inv_length[None, :]
    picked = jnp.concatenate([target * ROWS_DEV + jnp.arange(PANEL, dtype=jnp.int32) for target in range(3)])
    columns = scaled[picked]
    system = kernel_block(scaled, columns)
    all_ids = jnp.arange(configs, dtype=jnp.int32)
    winner, losing = (pairs[0], pairs[1])
    row_ids = jnp.concatenate([winner, losing, winner, losing, all_ids])
    col_ids = jnp.concatenate([winner, losing, losing, winner, all_ids])
    values = jnp.concatenate([weights, weights, -weights, -weights, nugget])
    system = system.at[row_ids, column_slots(col_ids, 0, ROWS_DEV, PANEL)].add(values, mode='drop')
    blocks = [system[:, target * PANEL:(target + 1) * PANEL] for target in range(3)]
    finished = jnp.zeros((configs,), dtype=bool)
    identity = jnp.eye(PANEL, dtype=jnp.float32)
    factors = []
    for source in range(2):
        current = blocks[source]
        first_row = source * ROWS_DEV
        lowest = jnp.linalg.cholesky(current[first_row:first_row + PANEL])
        inverse = jax.scipy.linalg.solve_triangular(lowest, identity, lower=True)
        factor = jnp.einsum('rk,jk->rj', current, inverse, precision=lax.Precision.HIGHEST)
        factor = factor.at[first_row:first_row + PANEL].set(lowest)
        factors.append(factor)
        finished = finished | (all_ids >= first_row) & (all_ids < first_row + PANEL)
        for target in range(source + 1, 3):
            shared = factor[target * ROWS_DEV:target * ROWS_DEV + PANEL]
            update = jnp.einsum('rk,jk->rj', factor, shared, precision=lax.Precision.HIGHEST)
            blocks[target] = jnp.where(finished[:, None], jnp.float32(0.0), blocks[target] - update)
    return (jnp.stack(factors), blocks[2])
```

```python
import jax
import jax.numpy as jnp
from jax import lax
from jax.experimental import pallas as pl
from jax.experimental.pallas import tpu as pltpu
from jax.sharding import PartitionSpec as P

PANEL = 512
ROWS_DEV = 4096
CONFIGS = 131072
BLOCK = 128
WINDOW = 12
CHAIN = 2 * PANEL
COLUMNS = CHAIN + BLOCK
ROW_STEP = 512
LOG2E = 1.4426950408889634
VMEM_BYTES = 56 * 1024 * 1024
HIGHEST = lax.Precision.HIGHEST
f32, bf16, i32 = jnp.float32, jnp.bfloat16, jnp.int32


def iota(shape, dim):
    return lax.broadcasted_iota(i32, shape, dim)


def dot_nt(left, right, precision=None):
    return lax.dot_general(
        left, right, (((1,), (1,)), ((), ())), precision=precision, preferred_element_type=f32
    )


def dot_nn(left, right, precision=None):
    return lax.dot_general(
        left, right, (((1,), (0,)), ((), ())), precision=precision, preferred_element_type=f32
    )


def split3(value):
    high = value.astype(bf16)
    rest = value - high.astype(f32)
    middle = rest.astype(bf16)
    low = (rest - middle.astype(f32)).astype(bf16)
    return high, middle, low


def split2(value):
    high = value.astype(bf16)
    return high, (value - high.astype(f32)).astype(bf16)


TABLE_CHUNK = 2048


def tables_kernel(pairs_ref, weights_ref, offc_ref, cc_ref, offr_ref, cr_ref, wl_ref, acc_ref):
    row = iota((40, 1), 0)
    code = row + 20 * ((row >= 12).astype(i32) + (row >= 24).astype(i32))
    code = jnp.where(row < 36, code, -1)
    low_id = iota((BLOCK, 1), 0)
    acc_ref[...] = jnp.zeros_like(acc_ref)

    def step(index, carry):
        span = pl.ds(pl.multiple_of(index * TABLE_CHUNK, TABLE_CHUNK), TABLE_CHUNK)
        winner = pairs_ref[0:1, span]
        loser = pairs_ref[1:2, span]
        weight = weights_ref[0:1, span]
        place = (winner + 1024) & (CONFIGS - 1)
        offset = (loser - winner) & (CONFIGS - 1)
        one_hot = jnp.where(low_id == (place & 127), f32(1.0), f32(0.0)).astype(bf16)
        hit = code == (place >> 7)
        parts = [(offset >> 5).astype(f32), (offset & 31).astype(f32)]
        parts += [part.astype(f32) for part in split3(weight)]
        values = [jnp.where(hit, part, f32(0.0)) for part in parts]
        values.append(jnp.zeros((8, TABLE_CHUNK), f32))
        acc_ref[:, 0:208] += dot_nt(one_hot, jnp.concatenate(values, 0).astype(bf16))
        return carry

    lax.fori_loop(0, CONFIGS // TABLE_CHUNK, step, 0)
    turned = acc_ref[...].T
    offr = (turned[0:40] * 32.0 + turned[40:80]).astype(i32)
    cr = turned[80:120] + turned[120:160] + turned[160:200]
    offr_ref[...] = offr
    cr_ref[...] = cr
    offc = jnp.concatenate([offr, jnp.zeros((88, BLOCK), i32)], 0).T
    cc = jnp.concatenate([cr, jnp.zeros((88, BLOCK), f32)], 0).T
    offc_ref[...] = offc
    cc_ref[...] = cc
    place = iota((BLOCK, 1), 0)
    lane = iota((BLOCK, BLOCK), 1)
    rows = []
    for panel in range(3):
        lost = [jnp.zeros((1, BLOCK), f32) for _ in range(4)]
        for h in range(12):
            r = panel * WINDOW + h
            target = jnp.broadcast_to(offc[:, r : r + 1] + (place + BLOCK * (h - 8)), (BLOCK, BLOCK)) - lane
            weight = jnp.broadcast_to(cc[:, r : r + 1], (BLOCK, BLOCK))
            for d in range(4):
                if h - 8 <= d:
                    found = jnp.where(target == BLOCK * d, weight, f32(0.0))
                    lost[d] = lost[d] + jnp.sum(found, axis=0, keepdims=True)
        for d in range(4):
            r = panel * WINDOW + 8 + d
            rows.append(lost[d] + cr[r : r + 1])
    rows.append(jnp.zeros((4, BLOCK), f32))
    wl_ref[...] = jnp.concatenate(rows, 0)


def pair_tables(pairs, weights):
    return pl.pallas_call(
        tables_kernel,
        name="pair_tables",
        out_shape=(
            jax.ShapeDtypeStruct((BLOCK, BLOCK), i32),
            jax.ShapeDtypeStruct((BLOCK, BLOCK), f32),
            jax.ShapeDtypeStruct((40, BLOCK), i32),
            jax.ShapeDtypeStruct((40, BLOCK), f32),
            jax.ShapeDtypeStruct((16, BLOCK), f32),
        ),
        scratch_shapes=[pltpu.VMEM((BLOCK, 256), f32)],
        compiler_params=pltpu.CompilerParams(vmem_limit_bytes=VMEM_BYTES),
        cost_estimate=pl.CostEstimate(
            flops=2 * CONFIGS * BLOCK * 256, bytes_accessed=12 * CONFIGS, transcendentals=0
        ),
    )(pairs, weights)


def hessian_block(first_row, first_col, own, partner, diagonal):
    row = iota((BLOCK, BLOCK), 0) + first_row
    col = iota((BLOCK, BLOCK), 1) + first_col
    own_offset, own_weight = own
    partner_offset, partner_weight = partner
    value = jnp.where(row + own_offset == col, -own_weight, f32(0.0))
    value = value + jnp.where(col + partner_offset == row, -partner_weight, f32(0.0))
    return value + jnp.where(row == col, diagonal, f32(0.0))


def factor_tiles(tiles):
    tiles = list(tiles)
    count = len(tiles)
    sub = iota((8, BLOCK), 0)
    lane = iota((8, BLOCK), 1)
    for k in range(count):
        base = 8 * k
        inside = (lane >= base) & (lane < base + 8)
        eye = jnp.where(lane == sub + base, f32(1.0), f32(0.0))
        cols = [jnp.broadcast_to(tiles[k][:, base + j : base + j + 1], (8, BLOCK)) for j in range(8)]
        entry = {}
        for j in range(8):
            for i in range(j, 8):
                entry[i, j] = jnp.broadcast_to(cols[j][i : i + 1, :], (8, BLOCK))
        own = jnp.where(inside, eye, tiles[k])
        inverse = []
        for j in range(8):
            scale = 1.0 / entry[j, j]
            inverse.append(scale)
            ratio = {i: entry[i, j] * scale for i in range(j + 1, 8)}
            for i in range(j + 1, 8):
                for m in range(j + 1, i + 1):
                    entry[i, m] = entry[i, m] - ratio[i] * entry[m, j]
            if j < 7:
                step = jnp.where(sub > j, cols[j] * scale, f32(0.0))
                for m in range(j + 1, 8):
                    cols[m] = cols[m] - step * entry[m, j]
                own = own - step * jnp.broadcast_to(own[j : j + 1, :], (8, BLOCK))
        rows = [jnp.broadcast_to(own[j : j + 1, :], (8, BLOCK)) for j in range(8)]
        for t in range(k + 1, count):
            tile = tiles[t]
            left = [jnp.broadcast_to(tile[:, base + j : base + j + 1], (8, BLOCK)) for j in range(8)]
            tile = jnp.where(inside, f32(0.0), tile)
            for j in range(8):
                step = left[j] * inverse[j]
                for m in range(j + 1, 8):
                    left[m] = left[m] - step * entry[m, j]
                tile = tile - step * rows[j]
            tiles[t] = tile
        scale = inverse[0]
        for j in range(1, 8):
            scale = jnp.where(sub == j, inverse[j], scale)
        tiles[k] = own * jnp.sqrt(scale)
    return tiles


def chain_kernel(
    rank_ref, g0_ref, g1_ref, g2_ref, g3_ref, p2_ref, inv_ref, offc_ref, cc_ref, offr_ref, cr_ref, wl_ref,
    mhi_ref, mlo_ref, b6_ref, csq_ref, dg_ref, x_ref, pts_ref, lower_ref,
):
    c = rank_ref[1]
    inv = inv_ref[...]
    dg_ref[...] = wl_ref[...]
    for k, g_ref in enumerate((g0_ref, g1_ref, g2_ref, g3_ref)):
        place = (c + k) & 3
        for panel in range(2):
            rows = pl.ds(pl.multiple_of(panel * PANEL + place * BLOCK, BLOCK), BLOCK)
            pts_ref[rows, :] = g_ref[panel * 136 : panel * 136 + BLOCK, :] * inv
            line = pl.ds(panel * 4 + place, 1)
            dg_ref[line, :] += g_ref[panel * 136 + BLOCK : panel * 136 + BLOCK + 1, :]
    pts_ref[CHAIN:COLUMNS, :] = p2_ref[0:BLOCK, :] * inv
    dg_ref[pl.ds(8 + c, 1), :] += p2_ref[BLOCK : BLOCK + 1, :]

    points = pts_ref[...]
    csq_ref[...] = 1.0 - (0.5 * LOG2E) * dot_nt(jnp.ones((8, BLOCK), f32), points * points, HIGHEST)
    bh, bm, bl = split3(points * LOG2E)
    b6_ref[...] = jnp.concatenate([bh, bm, bh, bm, bl, bh], 1)
    for k in range(8):
        rows = slice(k * BLOCK, (k + 1) * BLOCK)
        own = pts_ref[rows, :]
        own_sq = (-0.5 * LOG2E) * jnp.sum(own * own, axis=1, keepdims=True)
        ah, am, al = split3(own)
        inner = dot_nt(jnp.concatenate([ah, ah, am, am, ah, al], 1), b6_ref[k * BLOCK :, :])
        x_ref[rows, k * BLOCK :] = jnp.exp2(inner + (own_sq + csq_ref[0:1, k * BLOCK :]))
        if k:
            x_ref[rows, : k * BLOCK] = jnp.zeros((BLOCK, k * BLOCK), f32)
    for panel in range(2):
        for b in range(4):
            r = panel * WINDOW + 8 + b
            for d in range(b, 4):
                s = panel * WINDOW + 8 + d
                at = (
                    slice(panel * PANEL + b * BLOCK, panel * PANEL + (b + 1) * BLOCK),
                    slice(panel * PANEL + d * BLOCK, panel * PANEL + (d + 1) * BLOCK),
                )
                line = panel * 4 + d
                x_ref[at] += hessian_block(
                    b * BLOCK, d * BLOCK,
                    (offc_ref[:, r : r + 1], cc_ref[:, r : r + 1]),
                    (offr_ref[s : s + 1, :], cr_ref[s : s + 1, :]),
                    dg_ref[line : line + 1, :],
                )

    sub = iota((8, BLOCK), 0)
    lane = iota((8, BLOCK), 1)
    chunk = 384

    def panel_step(k, carry):
        first = pl.multiple_of(k * BLOCK, BLOCK)
        own = pl.ds(first, BLOCK)
        tiles = [x_ref[pl.ds(pl.multiple_of(first + 8 * t, 8), 8), own] for t in range(16)]
        for t, tile in enumerate(factor_tiles(tiles)):
            lower_ref[8 * t : 8 * t + 8, :] = jnp.where(lane <= sub + 8 * t, tile, f32(0.0))
            x_ref[pl.ds(pl.multiple_of(first + 8 * t, 8), 8), own] = jnp.where(
                lane == sub + 8 * t, f32(1.0), f32(0.0)
            )
        lower = lower_ref[...]
        for n in range(0, COLUMNS, chunk):
            x_ref[own, n : n + chunk] = dot_nn(lower, x_ref[own, n : n + chunk], HIGHEST)

        def trailing(i, inner_carry):
            rows = pl.ds(pl.multiple_of(i * BLOCK, BLOCK), BLOCK)
            turned = x_ref[own, rows].T
            x_ref[rows, own] = jnp.zeros((BLOCK, BLOCK), f32)
            for n in range(0, COLUMNS, chunk):
                x_ref[rows, n : n + chunk] -= dot_nn(turned, x_ref[own, n : n + chunk], HIGHEST)
            return inner_carry

        lax.fori_loop(k + 1, 8, trailing, 0)
        return carry

    lax.fori_loop(0, 8, panel_step, 0)

    wide = iota((BLOCK, CHAIN), 1)
    for panel in range(2):
        rows = pl.ds(pl.multiple_of(panel * PANEL + c * BLOCK, BLOCK), BLOCK)
        value = jnp.where(wide < panel * PANEL + (c + 1) * BLOCK, x_ref[rows, :CHAIN], f32(0.0))
        high, low = split2(value)
        mhi_ref[panel * BLOCK : (panel + 1) * BLOCK, :] = high
        mlo_ref[panel * BLOCK : (panel + 1) * BLOCK, :] = low
    turned = [x_ref[i * BLOCK : (i + 1) * BLOCK, CHAIN:].T for i in range(8)]
    for n in range(8):
        cols = slice(n * BLOCK, (n + 1) * BLOCK)
        value = jnp.zeros((BLOCK, BLOCK), f32)
        for i in range(n, 8):
            value = value - dot_nn(turned[i], x_ref[i * BLOCK : (i + 1) * BLOCK, cols], HIGHEST)
        high, low = split2(value)
        mhi_ref[2 * BLOCK :, cols] = high
        mlo_ref[2 * BLOCK :, cols] = low


def panel_chain(rank, gathered, third, inv_length, tables):
    vmem = pl.BlockSpec(memory_space=pltpu.VMEM)
    return pl.pallas_call(
        chain_kernel,
        name="panel_chain",
        in_specs=[pl.BlockSpec(memory_space=pltpu.SMEM)] + [vmem] * 11,
        out_shape=(
            jax.ShapeDtypeStruct((3 * BLOCK, CHAIN), bf16),
            jax.ShapeDtypeStruct((3 * BLOCK, CHAIN), bf16),
            jax.ShapeDtypeStruct((COLUMNS, 6 * BLOCK), bf16),
            jax.ShapeDtypeStruct((8, COLUMNS), f32),
            jax.ShapeDtypeStruct((16, BLOCK), f32),
        ),
        scratch_shapes=[
            pltpu.VMEM((CHAIN, COLUMNS), f32),
            pltpu.VMEM((COLUMNS, BLOCK), f32),
            pltpu.VMEM((BLOCK, BLOCK), f32),
        ],
        compiler_params=pltpu.CompilerParams(vmem_limit_bytes=VMEM_BYTES),
        cost_estimate=pl.CostEstimate(
            flops=8 * CHAIN * CHAIN * CHAIN, bytes_accessed=8 * 1024 * 1024, transcendentals=CHAIN * COLUMNS
        ),
    )(rank, *gathered, third, inv_length, *tables)


def rows_kernel(
    rank_ref, feat_ref, inv_ref, mhi_ref, mlo_ref, b6_ref, csq_ref, dg_ref, offc_ref, cc_ref, offr_ref, cr_ref,
    factor_ref, schur_ref, s_ref,
):
    r_rank = rank_ref[0]
    c = rank_ref[1]
    n = pl.program_id(0)
    own = feat_ref[...] * inv_ref[...]
    own_sq = (-0.5 * LOG2E) * jnp.sum(own * own, axis=1, keepdims=True)
    ah, am, al = split3(own)
    a6 = jnp.concatenate([ah, ah, am, am, ah, al], 1)
    for first in range(0, COLUMNS, 384):
        inner = dot_nt(a6, b6_ref[first : first + 384, :])
        s_ref[:, first : first + 384] = jnp.exp2(inner + (own_sq + csq_ref[0:1, first : first + 384]))

    def add_hessian(panel, start):
        lane = iota((BLOCK, BLOCK), 1)

        def per_row(b, carry):
            first_row = start + b * BLOCK
            r = panel * WINDOW + 8 + (start // BLOCK) + b
            pick = lane == r
            own_offset = jnp.sum(jnp.where(pick, offc_ref[...], 0), axis=1, keepdims=True)
            own_weight = jnp.sum(jnp.where(pick, cc_ref[...], f32(0.0)), axis=1, keepdims=True)
            own_weight = jnp.where(first_row < PANEL, own_weight, f32(0.0))

            def per_col(d, inner_carry):
                which = jnp.where(panel == 2, c, d)
                s = panel * WINDOW + 8 + which
                partner_weight = jnp.where(first_row >= 0, cr_ref[pl.ds(s, 1), :], f32(0.0))
                value = hessian_block(
                    first_row, which * BLOCK, (own_offset, own_weight),
                    (offr_ref[pl.ds(s, 1), :], partner_weight), dg_ref[pl.ds(panel * 4 + which, 1), :],
                )
                rows = pl.ds(pl.multiple_of(b * BLOCK, BLOCK), BLOCK)
                cols = pl.ds(pl.multiple_of(panel * PANEL + d * BLOCK, BLOCK), BLOCK)
                s_ref[rows, cols] += value
                return inner_carry

            lax.fori_loop(0, jnp.where(panel == 2, 1, 4), per_col, 0)
            return carry

        lax.fori_loop(0, ROW_STEP // BLOCK, per_row, 0)

    @pl.when((r_rank <= 2) & (n <= 2))
    def _():
        add_hessian(r_rank, n * ROW_STEP)

    following = jnp.where(r_rank == 31, 0, r_rank + 1)

    @pl.when((following <= 2) & (n >= 6))
    def _():
        add_hessian(following, (n - 8) * ROW_STEP)

    first_hi, first_lo = split2(s_ref[:, :PANEL])
    second_hi, second_lo = split2(s_ref[:, PANEL:CHAIN])

    def product(first_row, last_row, left, first_col):
        hi, lo = left
        cols = slice(first_col, first_col + PANEL)
        rows = slice(first_row, last_row)
        return (
            dot_nt(hi, mhi_ref[rows, cols]) + dot_nt(lo, mhi_ref[rows, cols]) + dot_nt(hi, mlo_ref[rows, cols])
        )

    from_first = product(0, 3 * BLOCK, (first_hi, first_lo), 0)
    from_second = product(BLOCK, 3 * BLOCK, (second_hi, second_lo), PANEL)
    keep_second = jnp.where((r_rank == 0) & (n == 0), f32(0.0), f32(1.0))
    keep_schur = jnp.where((r_rank <= 1) & (n == 0), f32(0.0), f32(1.0))
    factor_ref[0] = from_first[:, :BLOCK]
    factor_ref[1] = (from_first[:, BLOCK : 2 * BLOCK] + from_second[:, :BLOCK]) * keep_second
    schur_ref[...] = (s_ref[:, CHAIN:] + from_first[:, 2 * BLOCK :] + from_second[:, BLOCK:]) * keep_schur


def own_rows(rank, features, inv_length, chain, tables):
    def whole(shape):
        return pl.BlockSpec(shape, lambda n: (0, 0))

    offc, cc, offr, cr, _ = tables
    return pl.pallas_call(
        rows_kernel,
        name="own_rows",
        grid=(ROWS_DEV // ROW_STEP,),
        in_specs=[
            pl.BlockSpec(memory_space=pltpu.SMEM),
            pl.BlockSpec((ROW_STEP, BLOCK), lambda n: (n, 0)),
            whole((1, BLOCK)),
            whole((3 * BLOCK, CHAIN)),
            whole((3 * BLOCK, CHAIN)),
            whole((COLUMNS, 6 * BLOCK)),
            whole((8, COLUMNS)),
            whole((16, BLOCK)),
            whole((BLOCK, BLOCK)),
            whole((BLOCK, BLOCK)),
            whole((40, BLOCK)),
            whole((40, BLOCK)),
        ],
        out_specs=(
            pl.BlockSpec((2, ROW_STEP, BLOCK), lambda n: (0, n, 0)),
            pl.BlockSpec((ROW_STEP, BLOCK), lambda n: (n, 0)),
        ),
        out_shape=(
            jax.ShapeDtypeStruct((2, ROWS_DEV, BLOCK), f32),
            jax.ShapeDtypeStruct((ROWS_DEV, BLOCK), f32),
        ),
        scratch_shapes=[pltpu.VMEM((ROW_STEP, COLUMNS), f32)],
        compiler_params=pltpu.CompilerParams(vmem_limit_bytes=VMEM_BYTES),
        cost_estimate=pl.CostEstimate(
            flops=2 * ROWS_DEV * COLUMNS * 768 + 6 * ROWS_DEV * CHAIN * 384,
            bytes_accessed=12 * 1024 * 1024,
            transcendentals=ROWS_DEV * COLUMNS,
        ),
    )(rank, features, inv_length, *chain, offc, cc, offr, cr)


def row_index(z, y, core):
    return (z % 4) * 8 + (y % 4) * 2 + core


def share_panels(features, nugget):
    row = lax.axis_index("row")
    col = lax.axis_index("col")
    z, y, core = row // 8, (row // 2) % 4, row % 2
    quarter = lax.dynamic_slice_in_dim(features, col * BLOCK, BLOCK, 0)
    extra = lax.dynamic_slice_in_dim(nugget, col * BLOCK, BLOCK, 0)[None, :]
    mine = jnp.concatenate([quarter, jnp.broadcast_to(extra, (8, BLOCK))], 0)

    def send(value, pairs):
        return lax.ppermute(value, "row", pairs)

    along_z = [
        send(mine, [(row_index(0, *at), row_index(k, *at)) for at in ((0, 0), (0, 1), (1, 0))]) for k in (1, 2, 3)
    ]
    for k in (1, 2, 3):
        mine = jnp.where(z == k, along_z[k - 1], mine)
    along_y = [
        send(
            mine,
            [
                (row_index(k, at, half), row_index(k, at + s, half))
                for k in range(4)
                for at, half in ((0, 0), (0, 1), (1, 0))
            ],
        )
        for s in (1, 2, 3)
    ]
    first, third = mine, mine
    for s in (1, 2, 3):
        first = jnp.where(y == s, along_y[s - 1], first)
        third = jnp.where(y == (1 + s) % 4, along_y[s - 1], third)
    other = send(jnp.concatenate([first, third], 0), [(i, i ^ 1) for i in range(32)])
    low = core == 0
    pair = jnp.concatenate([jnp.where(low, first, other[:136]), jnp.where(low, other[:136], first)], 0)
    third = jnp.where(low, third, other[136:])
    gathered = [pair] + [lax.ppermute(pair, "col", [((i + k) % 4, i) for i in range(4)]) for k in (1, 2, 3)]
    return gathered, third


def per_device(features, inv_length, nugget, pairs, weights):
    rank = jnp.stack([lax.axis_index("row"), lax.axis_index("col")]).astype(i32)
    inv_length = inv_length.reshape(1, BLOCK)
    gathered, third = share_panels(features, nugget)
    tables = pair_tables(pairs, weights.reshape(1, CONFIGS))
    chain = panel_chain(rank, gathered, third, inv_length, tables)
    return own_rows(rank, features, inv_length, chain, tables)


def solution(mesh):
    placed = (P("row", None), P(), P("row"), P(), P())
    return jax.shard_map(
        per_device,
        mesh=mesh,
        in_specs=placed,
        out_specs=(P(None, "row", "col"), P("row", "col")),
        check_vma=False,
    )
```

```python
import jax
import jax.numpy as jnp
from jax import lax
from jax.experimental import pallas as pl
from jax.experimental.pallas import tpu as pltpu
from jax.sharding import PartitionSpec as P

PANEL = 512
ROWS_DEV = 4096
CONFIGS = 131072
BLOCK = 128
WINDOW = 12
CHAIN = 2 * PANEL
COLUMNS = CHAIN + BLOCK
ROW_STEP = 512
ROW_STEPS = ROWS_DEV // ROW_STEP
ROOT_LOG2E = 1.2011224087864498
VMEM_BYTES = 56 * 1024 * 1024
HIGHEST = lax.Precision.HIGHEST
f32, bf16, i32 = jnp.float32, jnp.bfloat16, jnp.int32


def iota(shape, dim):
    return lax.broadcasted_iota(i32, shape, dim)


def dot_nt(left, right, precision=None):
    return lax.dot_general(
        left, right, (((1,), (1,)), ((), ())), precision=precision, preferred_element_type=f32
    )


def dot_nn(left, right, precision=None):
    return lax.dot_general(
        left, right, (((1,), (0,)), ((), ())), precision=precision, preferred_element_type=f32
    )


def split3(value):
    high = value.astype(bf16)
    rest = value - high.astype(f32)
    middle = rest.astype(bf16)
    low = (rest - middle.astype(f32)).astype(bf16)
    return high, middle, low


def split2(value):
    high = value.astype(bf16)
    return high, (value - high.astype(f32)).astype(bf16)


TABLE_CHUNK = 2048
TABLE_ROWS = 96
QUARTER = BLOCK + 8


def tables_kernel(rank_ref, pairs_ref, weights_ref, out_ref, acc_ref):
    row = iota((40, 1), 0)
    code = row + 20 * ((row >= 12).astype(i32) + (row >= 24).astype(i32))
    code = jnp.where(row < 36, code, -1)
    low_id = iota((BLOCK, 1), 0)
    acc_ref[...] = jnp.zeros_like(acc_ref)
    share = CONFIGS // 8
    start = (2 * rank_ref[1] + (rank_ref[0] & 1)) * share

    def step(index, carry):
        span = pl.ds(pl.multiple_of(start + index * TABLE_CHUNK, TABLE_CHUNK), TABLE_CHUNK)
        winner = pairs_ref[0:1, span]
        loser = pairs_ref[1:2, span]
        weight = weights_ref[0:1, span]
        place = (winner + 1024) & (CONFIGS - 1)
        offset = (loser - winner) & (CONFIGS - 1)
        one_hot = jnp.where(low_id == (place & 127), f32(1.0), f32(0.0)).astype(bf16)
        hit = code == (place >> 7)
        parts = [(offset >> 5).astype(f32), (offset & 31).astype(f32)]
        parts += [part.astype(f32) for part in split3(weight)]
        values = [jnp.where(hit, part, f32(0.0)) for part in parts]
        values.append(jnp.zeros((8, TABLE_CHUNK), f32))
        acc_ref[:, 0:208] += dot_nt(one_hot, jnp.concatenate(values, 0).astype(bf16))
        return carry

    lax.fori_loop(0, share // TABLE_CHUNK, step, 0)
    turned = acc_ref[...].T
    offr = turned[0:40] * 32.0 + turned[40:80]
    cr = turned[80:120] + turned[120:160] + turned[160:200]
    out_ref[0:40, :] = offr
    out_ref[40:80, :] = cr
    offc = jnp.concatenate([offr.astype(i32), jnp.zeros((88, BLOCK), i32)], 0).T
    cc = jnp.concatenate([cr, jnp.zeros((88, BLOCK), f32)], 0).T
    place = iota((BLOCK, 1), 0)
    lane = iota((BLOCK, BLOCK), 1)
    rows = []
    for panel in range(3):
        lost = [jnp.zeros((1, BLOCK), f32) for _ in range(4)]
        for h in range(12):
            r = panel * WINDOW + h
            target = jnp.broadcast_to(offc[:, r : r + 1] + (place + BLOCK * (h - 8)), (BLOCK, BLOCK)) - lane
            weight = jnp.broadcast_to(cc[:, r : r + 1], (BLOCK, BLOCK))
            for d in range(4):
                if h - 8 <= d:
                    found = jnp.where(target == BLOCK * d, weight, f32(0.0))
                    lost[d] = lost[d] + jnp.sum(found, axis=0, keepdims=True)
        for d in range(4):
            r = panel * WINDOW + 8 + d
            rows.append(lost[d] + cr[r : r + 1])
    rows.append(jnp.zeros((4, BLOCK), f32))
    out_ref[80:96, :] = jnp.concatenate(rows, 0)


def pair_tables(rank, pairs, weights):
    vmem = pl.BlockSpec(memory_space=pltpu.VMEM)
    return pl.pallas_call(
        tables_kernel,
        name="pair_tables",
        in_specs=[pl.BlockSpec(memory_space=pltpu.SMEM), vmem, vmem],
        out_shape=jax.ShapeDtypeStruct((TABLE_ROWS, BLOCK), f32),
        scratch_shapes=[pltpu.VMEM((BLOCK, 256), f32)],
        compiler_params=pltpu.CompilerParams(vmem_limit_bytes=VMEM_BYTES),
        cost_estimate=pl.CostEstimate(
            flops=2 * CONFIGS * BLOCK * 256, bytes_accessed=12 * CONFIGS, transcendentals=0
        ),
    )(rank, pairs, weights)


def hessian_block(first_row, first_col, own, partner, diagonal):
    row = iota((BLOCK, BLOCK), 0) + first_row
    col = iota((BLOCK, BLOCK), 1) + first_col
    own_offset, own_weight = own
    partner_offset, partner_weight = partner
    value = jnp.where(row + own_offset == col, -own_weight, f32(0.0))
    value = value + jnp.where(col + partner_offset == row, -partner_weight, f32(0.0))
    return value + jnp.where(row == col, diagonal, f32(0.0))


def factor_tiles(tiles):
    tiles = list(tiles)
    count = len(tiles)
    sub = iota((8, BLOCK), 0)
    lane = iota((8, BLOCK), 1)
    for k in range(count):
        base = 8 * k
        inside = (lane >= base) & (lane < base + 8)
        eye = jnp.where(lane == sub + base, f32(1.0), f32(0.0))
        cols = [jnp.broadcast_to(tiles[k][:, base + j : base + j + 1], (8, BLOCK)) for j in range(8)]
        entry = {}
        for j in range(8):
            for i in range(j, 8):
                entry[i, j] = jnp.broadcast_to(cols[j][i : i + 1, :], (8, BLOCK))
        own = jnp.where(inside, eye, tiles[k])
        inverse = []
        for j in range(8):
            scale = 1.0 / entry[j, j]
            inverse.append(scale)
            ratio = {i: entry[i, j] * scale for i in range(j + 1, 8)}
            for i in range(j + 1, 8):
                for m in range(j + 1, i + 1):
                    entry[i, m] = entry[i, m] - ratio[i] * entry[m, j]
            if j < 7:
                step = jnp.where(sub > j, cols[j] * scale, f32(0.0))
                for m in range(j + 1, 8):
                    cols[m] = cols[m] - step * entry[m, j]
                own = own - step * jnp.broadcast_to(own[j : j + 1, :], (8, BLOCK))
        rows = [jnp.broadcast_to(own[j : j + 1, :], (8, BLOCK)) for j in range(8)]
        for t in range(k + 1, count):
            tile = tiles[t]
            left = [jnp.broadcast_to(tile[:, base + j : base + j + 1], (8, BLOCK)) for j in range(8)]
            tile = jnp.where(inside, f32(0.0), tile)
            for j in range(8):
                step = left[j] * inverse[j]
                for m in range(j + 1, 8):
                    left[m] = left[m] - step * entry[m, j]
                tile = tile - step * rows[j]
            tiles[t] = tile
        scale = inverse[0]
        for j in range(1, 8):
            scale = jnp.where(sub == j, inverse[j], scale)
        tiles[k] = own * jnp.sqrt(scale)
    return tiles


def dot3(left, right):
    lh, ll = left
    rh, rl = right
    return dot_nn(lh, rh) + (dot_nn(lh, rl) + dot_nn(ll, rh))


def points_parts(value, scale):
    high, middle = split2(value * scale)
    return high, middle, high.astype(f32) + middle.astype(f32)


def chain_kernel(
    rank_ref, mine_ref, other_ref, inv_ref, feat_ref, factor_hbm, schur_hbm,
    x_ref, dg_ref, offc_ref, cc_ref, offr_ref, cr_ref, b4_ref, csq_ref, pts_ref, t_ref, lower_ref, d_ref,
    wh_ref, wl_ref, uh_ref, ul_ref, sh_ref, sl_ref, s2_ref, mh_ref, ml_ref, out_ref, out_sem,
):
    r_rank = rank_ref[0]
    c = rank_ref[1]
    even = (r_rank & 1) == 0
    scale = inv_ref[...] * ROOT_LOG2E

    def of_panel(panel, rows):
        return jnp.where(even == (panel != 1), mine_ref[rows, :], other_ref[rows, :])

    at = slice(4 * QUARTER, 4 * QUARTER + TABLE_ROWS)
    table = mine_ref[at, :] + other_ref[at, :]
    offr = table[0:40].astype(i32)
    cr = table[40:80]
    offr_ref[...] = offr
    cr_ref[...] = cr
    offc_ref[...] = jnp.concatenate([offr, jnp.zeros((88, BLOCK), i32)], 0).T
    cc_ref[...] = jnp.concatenate([cr, jnp.zeros((88, BLOCK), f32)], 0).T
    dg_ref[...] = table[80:96]
    for k in range(4):
        place = (c + k) & 3
        first = k * QUARTER
        for panel in range(2):
            rows = pl.ds(pl.multiple_of(panel * PANEL + place * BLOCK, BLOCK), BLOCK)
            pts_ref[rows, :] = of_panel(panel, slice(first, first + BLOCK))
            dg_ref[pl.ds(panel * 4 + place, 1), :] += of_panel(panel, slice(first + BLOCK, first + BLOCK + 1))
    first = 4 * QUARTER + TABLE_ROWS
    pts_ref[CHAIN:COLUMNS, :] = of_panel(2, slice(first, first + BLOCK))
    dg_ref[pl.ds(8 + c, 1), :] += of_panel(2, slice(first + BLOCK, first + BLOCK + 1))

    for k in range(9):
        cols = slice(k * BLOCK, (k + 1) * BLOCK)
        high, middle, near = points_parts(pts_ref[cols, :], scale)
        near = near.T
        csq_ref[:, cols] = jnp.broadcast_to(1.0 - 0.5 * jnp.sum(near * near, axis=0, keepdims=True), (8, BLOCK))
        high, middle = split2(near)
        for n, part in enumerate((high, middle, high, middle)):
            b4_ref[n * BLOCK : (n + 1) * BLOCK, cols] = part

    def kernel_rows(value, cols):
        high, middle, near = points_parts(value, scale)
        own_sq = -0.5 * jnp.sum(near * near, axis=1, keepdims=True)
        inner = dot_nn(jnp.concatenate([high, high, middle, middle], 1), b4_ref[:, cols])
        return jnp.exp2(inner + (own_sq + csq_ref[0:1, cols]))

    for k in range(8):
        rows = slice(k * BLOCK, (k + 1) * BLOCK)
        x_ref[rows, k * BLOCK :] = kernel_rows(pts_ref[rows, :], slice(k * BLOCK, COLUMNS))
        if k:
            x_ref[rows, : k * BLOCK] = jnp.zeros((BLOCK, k * BLOCK), f32)
    for ref in (wh_ref, wl_ref, uh_ref, ul_ref, t_ref, lower_ref):
        ref[...] = jnp.zeros_like(ref)
    for panel in range(2):
        for b in range(4):
            r = panel * WINDOW + 8 + b
            for d in range(b, 4):
                s = panel * WINDOW + 8 + d
                at = (
                    slice(panel * PANEL + b * BLOCK, panel * PANEL + (b + 1) * BLOCK),
                    slice(panel * PANEL + d * BLOCK, panel * PANEL + (d + 1) * BLOCK),
                )
                line = panel * 4 + d
                x_ref[at] += hessian_block(
                    b * BLOCK, d * BLOCK,
                    (offc_ref[:, r : r + 1], cc_ref[:, r : r + 1]),
                    (offr_ref[s : s + 1, :], cr_ref[s : s + 1, :]),
                    dg_ref[line : line + 1, :],
                )

    sub = iota((8, BLOCK), 0)
    lane = iota((8, BLOCK), 1)
    d_ref[...] = x_ref[:BLOCK, :BLOCK]

    def block_rows(index):
        return pl.ds(pl.multiple_of(index * BLOCK, BLOCK), BLOCK)

    def finish_row(k):
        own = block_rows(k)
        row = dot3(split2(lower_ref[...]), split2(t_ref[...]))
        high, low = split2(row)
        wh_ref[:, own] = jnp.zeros((CHAIN, BLOCK), bf16)
        wl_ref[:, own] = jnp.zeros((CHAIN, BLOCK), bf16)
        wh_ref[own, :] = high
        wl_ref[own, :] = low
        for i in range(1, 8):
            turned_high, turned_low = split2(row[:, i * BLOCK : (i + 1) * BLOCK].T)
            uh_ref[i * BLOCK : (i + 1) * BLOCK, own] = turned_high
            ul_ref[i * BLOCK : (i + 1) * BLOCK, own] = turned_low

    def panel_step(k, carry):
        own = block_rows(k)
        following = jnp.minimum(k + 1, 7)
        after = block_rows(following)
        tiles = factor_tiles([d_ref[8 * t : 8 * t + 8, :] for t in range(16)])

        finish_row(jnp.maximum(k - 1, 0))
        left = (uh_ref[own, :], ul_ref[own, :])
        t_ref[...] = x_ref[own, :] - dot3(left, (wh_ref[...], wl_ref[...]))
        for t in range(16):
            t_ref[8 * t : 8 * t + 8, own] = jnp.where(lane == sub + 8 * t, f32(1.0), f32(0.0))
        left = (uh_ref[after, :], ul_ref[after, :])
        block = x_ref[after, after] - dot3(left, (wh_ref[:, after], wl_ref[:, after]))

        rows = pl.ds(pl.multiple_of(k * ROW_STEP, ROW_STEP), ROW_STEP)
        value = kernel_rows(feat_ref[rows, :], slice(0, COLUMNS))
        high, low = split2(value[:, :CHAIN])
        sh_ref[rows, :] = high
        sl_ref[rows, :] = low
        s2_ref[rows, :] = value[:, CHAIN:]

        lower = jnp.concatenate([jnp.where(lane <= sub + 8 * t, tiles[t], f32(0.0)) for t in range(16)], 0)
        lower_ref[...] = lower
        upper = dot3(split2(lower), split2(t_ref[:, after]))
        d_ref[...] = block - dot3(split2(upper.T), split2(upper))
        return carry

    lax.fori_loop(0, 8, panel_step, 0)
    finish_row(7)

    def add_hessian(panel, start):
        wide = iota((BLOCK, BLOCK), 1)

        def per_row(b, carry):
            first_row = start + b * BLOCK
            r = panel * WINDOW + 8 + (start // BLOCK) + b
            pick = wide == r
            own_offset = jnp.sum(jnp.where(pick, offc_ref[...], 0), axis=1, keepdims=True)
            own_weight = jnp.sum(jnp.where(pick, cc_ref[...], f32(0.0)), axis=1, keepdims=True)
            own_weight = jnp.where(first_row < PANEL, own_weight, f32(0.0))
            rows = block_rows(jnp.where(start < 0, b + (ROWS_DEV + start) // BLOCK, b + start // BLOCK))

            def value_at(which):
                s = panel * WINDOW + 8 + which
                partner_weight = jnp.where(first_row >= 0, cr_ref[pl.ds(s, 1), :], f32(0.0))
                return hessian_block(
                    first_row, which * BLOCK, (own_offset, own_weight),
                    (offr_ref[pl.ds(s, 1), :], partner_weight), dg_ref[pl.ds(panel * 4 + which, 1), :],
                )

            @pl.when(panel == 2)
            def _():
                s2_ref[rows, :] += value_at(c)

            @pl.when(panel < 2)
            def _():
                for d in range(4):
                    cols = pl.ds(pl.multiple_of(panel * PANEL + d * BLOCK, BLOCK), BLOCK)
                    value = sh_ref[rows, cols].astype(f32) + sl_ref[rows, cols].astype(f32) + value_at(d)
                    high, low = split2(value)
                    sh_ref[rows, cols] = high
                    sl_ref[rows, cols] = low

            return carry

        lax.fori_loop(0, jnp.where(start < 0, 8, 12), per_row, 0)

    @pl.when(r_rank <= 2)
    def _():
        add_hessian(r_rank, 0)

    next_panel = jnp.where(r_rank == 31, 0, r_rank + 1)

    @pl.when(next_panel <= 2)
    def _():
        add_hessian(next_panel, -1024)

    for panel in range(2):
        rows = pl.ds(pl.multiple_of(panel * PANEL + c * BLOCK, BLOCK), BLOCK)
        value = wh_ref[rows, :CHAIN].astype(f32) + wl_ref[rows, :CHAIN].astype(f32)
        for n in range(8):
            high, low = split2(value[:, n * BLOCK : (n + 1) * BLOCK].T)
            mh_ref[n * BLOCK : (n + 1) * BLOCK, panel * BLOCK : (panel + 1) * BLOCK] = high
            ml_ref[n * BLOCK : (n + 1) * BLOCK, panel * BLOCK : (panel + 1) * BLOCK] = low
    turned = jnp.concatenate(
        [
            (wh_ref[rows, CHAIN:].astype(f32) + wl_ref[rows, CHAIN:].astype(f32)).T
            for rows in (slice(i * BLOCK, (i + 1) * BLOCK) for i in range(8))
        ],
        1,
    )
    value = dot3(split2(turned), (wh_ref[:, :CHAIN], wl_ref[:, :CHAIN]))
    for n in range(8):
        high, low = split2(-value[:, n * BLOCK : (n + 1) * BLOCK].T)
        mh_ref[n * BLOCK : (n + 1) * BLOCK, 2 * BLOCK :] = high
        ml_ref[n * BLOCK : (n + 1) * BLOCK, 2 * BLOCK :] = low

    def copies(n):
        rows = pl.ds(pl.multiple_of(n * ROW_STEP, ROW_STEP), ROW_STEP)
        return [
            pltpu.make_async_copy(out_ref.at[0, rows], factor_hbm.at[0, rows], out_sem.at[n, 0]),
            pltpu.make_async_copy(out_ref.at[1, rows], factor_hbm.at[1, rows], out_sem.at[n, 1]),
            pltpu.make_async_copy(out_ref.at[2, rows], schur_hbm.at[rows], out_sem.at[n, 2]),
        ]

    def out_step(n, carry):
        rows = pl.ds(pl.multiple_of(n * ROW_STEP, ROW_STEP), ROW_STEP)
        both = (sh_ref[rows, :], sl_ref[rows, :])
        rest = dot3(both, (mh_ref[:, BLOCK:], ml_ref[:, BLOCK:]))
        both = (sh_ref[rows, :PANEL], sl_ref[rows, :PANEL])
        head = dot3(both, (mh_ref[:PANEL, :BLOCK], ml_ref[:PANEL, :BLOCK]))
        keep_second = jnp.where((r_rank == 0) & (n == 0), f32(0.0), f32(1.0))
        keep_schur = jnp.where((r_rank <= 1) & (n == 0), f32(0.0), f32(1.0))
        out_ref[0, rows, :] = head
        out_ref[1, rows, :] = rest[:, :BLOCK] * keep_second
        out_ref[2, rows, :] = (s2_ref[rows, :] + rest[:, BLOCK:]) * keep_schur
        for copy in copies(n):
            copy.start()
        return carry

    lax.fori_loop(0, ROW_STEPS, out_step, 0)
    for n in range(ROW_STEPS):
        for copy in copies(n):
            copy.wait()


def panel_chain(rank, mine, other, inv_length, features):
    vmem = pl.BlockSpec(memory_space=pltpu.VMEM)
    anywhere = pl.BlockSpec(memory_space=pl.ANY)
    return pl.pallas_call(
        chain_kernel,
        name="panel_chain",
        in_specs=[pl.BlockSpec(memory_space=pltpu.SMEM)] + [vmem] * 4,
        out_specs=(anywhere, anywhere),
        out_shape=(
            jax.ShapeDtypeStruct((2, ROWS_DEV, BLOCK), f32),
            jax.ShapeDtypeStruct((ROWS_DEV, BLOCK), f32),
        ),
        scratch_shapes=[
            pltpu.VMEM((CHAIN, COLUMNS), f32),
            pltpu.VMEM((16, BLOCK), f32),
            pltpu.VMEM((BLOCK, BLOCK), i32),
            pltpu.VMEM((BLOCK, BLOCK), f32),
            pltpu.VMEM((40, BLOCK), i32),
            pltpu.VMEM((40, BLOCK), f32),
            pltpu.VMEM((PANEL, COLUMNS), bf16),
            pltpu.VMEM((8, COLUMNS), f32),
            pltpu.VMEM((COLUMNS, BLOCK), f32),
            pltpu.VMEM((BLOCK, COLUMNS), f32),
            pltpu.VMEM((BLOCK, BLOCK), f32),
            pltpu.VMEM((BLOCK, BLOCK), f32),
            pltpu.VMEM((CHAIN, COLUMNS), bf16),
            pltpu.VMEM((CHAIN, COLUMNS), bf16),
            pltpu.VMEM((CHAIN, CHAIN), bf16),
            pltpu.VMEM((CHAIN, CHAIN), bf16),
            pltpu.VMEM((ROWS_DEV, CHAIN), bf16),
            pltpu.VMEM((ROWS_DEV, CHAIN), bf16),
            pltpu.VMEM((ROWS_DEV, BLOCK), f32),
            pltpu.VMEM((CHAIN, 3 * BLOCK), bf16),
            pltpu.VMEM((CHAIN, 3 * BLOCK), bf16),
            pltpu.VMEM((3, ROWS_DEV, BLOCK), f32),
            pltpu.SemaphoreType.DMA((ROW_STEPS, 3)),
        ],
        compiler_params=pltpu.CompilerParams(vmem_limit_bytes=VMEM_BYTES),
        cost_estimate=pl.CostEstimate(
            flops=6 * ROWS_DEV * COLUMNS * CHAIN, bytes_accessed=12 * 1024 * 1024, transcendentals=ROWS_DEV * COLUMNS
        ),
    )(rank, mine, other, inv_length, features)


def row_index(z, y, core):
    return (z % 4) * 8 + (y % 4) * 2 + core


def share_panels(features, nugget, tables):
    row = lax.axis_index("row")
    col = lax.axis_index("col")
    z, y = row // 8, (row // 2) % 4
    quarter = lax.dynamic_slice_in_dim(features, col * BLOCK, BLOCK, 0)
    extra = lax.dynamic_slice_in_dim(nugget, col * BLOCK, BLOCK, 0)[None, :]
    mine = jnp.concatenate([quarter, jnp.broadcast_to(extra, (8, BLOCK))], 0)

    def send(value, pairs):
        return lax.ppermute(value, "row", pairs)

    along_z = [
        send(mine, [(row_index(0, *at), row_index(k, *at)) for at in ((0, 0), (0, 1), (1, 0))]) for k in (1, 2, 3)
    ]
    for k in (1, 2, 3):
        mine = jnp.where(z == k, along_z[k - 1], mine)
    along_y = [
        send(
            mine,
            [
                (row_index(k, at, half), row_index(k, at + s, half))
                for k in range(4)
                for at, half in ((0, 0), (0, 1), (1, 0))
            ],
        )
        for s in (1, 2, 3)
    ]
    first, third = mine, mine
    for s in (1, 2, 3):
        first = jnp.where(y == s, along_y[s - 1], first)
        third = jnp.where(y == (1 + s) % 4, along_y[s - 1], third)
    part = jnp.concatenate([first, tables], 0)
    parts = [part] + [lax.ppermute(part, "col", [((i + k) % 4, i) for i in range(4)]) for k in (1, 2, 3)]
    summed = (parts[0][QUARTER:] + parts[1][QUARTER:]) + (parts[2][QUARTER:] + parts[3][QUARTER:])
    held = jnp.concatenate([part[:QUARTER] for part in parts] + [summed, third], 0)
    return held, send(held, [(i, i ^ 1) for i in range(32)])


def per_device(features, inv_length, nugget, pairs, weights):
    rank = jnp.stack([lax.axis_index("row"), lax.axis_index("col")]).astype(i32)
    tables = pair_tables(rank, pairs, weights.reshape(1, CONFIGS))
    mine, other = share_panels(features, nugget, tables)
    return panel_chain(rank, mine, other, inv_length.reshape(1, BLOCK), features)


def solution(mesh):
    placed = (P("row", None), P(), P("row"), P(), P())
    return jax.shard_map(
        per_device,
        mesh=mesh,
        in_specs=placed,
        out_specs=(P(None, "row", "col"), P("row", "col")),
        check_vma=False,
    )
```

```python
import functools

import jax
import jax.numpy as jnp
from jax import lax
from jax.experimental import pallas as pl
from jax.experimental.pallas import tpu as pltpu
from jax.sharding import PartitionSpec as P

PANEL = 512
ROWS_DEV = 4096
CONFIGS = 131072
BLOCK = 128
WINDOW = 12
CHAIN = 2 * PANEL
COLUMNS = CHAIN + BLOCK
ROW_STEP = 512
ROW_STEPS = ROWS_DEV // ROW_STEP
ROOT_LOG2E = 1.2011224087864498
VMEM_BYTES = 56 * 1024 * 1024
HIGHEST = lax.Precision.HIGHEST
f32, bf16, i32 = jnp.float32, jnp.bfloat16, jnp.int32


def iota(shape, dim):
    return lax.broadcasted_iota(i32, shape, dim)


def dot_nt(left, right, precision=None):
    return lax.dot_general(
        left, right, (((1,), (1,)), ((), ())), precision=precision, preferred_element_type=f32
    )


def dot_nn(left, right, precision=None):
    return lax.dot_general(
        left, right, (((1,), (0,)), ((), ())), precision=precision, preferred_element_type=f32
    )


def split3(value):
    high = value.astype(bf16)
    rest = value - high.astype(f32)
    middle = rest.astype(bf16)
    low = (rest - middle.astype(f32)).astype(bf16)
    return high, middle, low


def split2(value):
    high = value.astype(bf16)
    return high, (value - high.astype(f32)).astype(bf16)


TABLE_CHUNK = 2048
TABLE_ROWS = 96
QUARTER = BLOCK + 8


def tables_kernel(rank_ref, pairs_ref, weights_ref, out_ref, acc_ref):
    row = iota((40, 1), 0)
    code = row + 20 * ((row >= 12).astype(i32) + (row >= 24).astype(i32))
    code = jnp.where(row < 36, code, -1)
    low_id = iota((BLOCK, 1), 0)
    acc_ref[...] = jnp.zeros_like(acc_ref)
    share = CONFIGS // 8
    start = (2 * rank_ref[1] + (rank_ref[0] & 1)) * share

    def step(index, carry):
        span = pl.ds(pl.multiple_of(start + index * TABLE_CHUNK, TABLE_CHUNK), TABLE_CHUNK)
        winner = pairs_ref[0:1, span]
        loser = pairs_ref[1:2, span]
        weight = weights_ref[0:1, span]
        place = (winner + 1024) & (CONFIGS - 1)
        offset = (loser - winner) & (CONFIGS - 1)
        one_hot = jnp.where(low_id == (place & 127), f32(1.0), f32(0.0)).astype(bf16)
        hit = code == (place >> 7)
        parts = [(offset >> 5).astype(f32), (offset & 31).astype(f32)]
        parts += [part.astype(f32) for part in split3(weight)]
        values = [jnp.where(hit, part, f32(0.0)) for part in parts]
        values.append(jnp.zeros((8, TABLE_CHUNK), f32))
        acc_ref[:, 0:208] += dot_nt(one_hot, jnp.concatenate(values, 0).astype(bf16))
        return carry

    lax.fori_loop(0, share // TABLE_CHUNK, step, 0)
    turned = acc_ref[...].T
    offr = turned[0:40] * 32.0 + turned[40:80]
    cr = turned[80:120] + turned[120:160] + turned[160:200]
    out_ref[0:40, :] = offr
    out_ref[40:80, :] = cr
    offc = jnp.concatenate([offr.astype(i32), jnp.zeros((88, BLOCK), i32)], 0).T
    cc = jnp.concatenate([cr, jnp.zeros((88, BLOCK), f32)], 0).T
    place = iota((BLOCK, 1), 0)
    lane = iota((BLOCK, BLOCK), 1)
    rows = []
    for panel in range(3):
        lost = [jnp.zeros((1, BLOCK), f32) for _ in range(4)]
        for h in range(12):
            r = panel * WINDOW + h
            target = jnp.broadcast_to(offc[:, r : r + 1] + (place + BLOCK * (h - 8)), (BLOCK, BLOCK)) - lane
            weight = jnp.broadcast_to(cc[:, r : r + 1], (BLOCK, BLOCK))
            for d in range(4):
                if h - 8 <= d:
                    found = jnp.where(target == BLOCK * d, weight, f32(0.0))
                    lost[d] = lost[d] + jnp.sum(found, axis=0, keepdims=True)
        for d in range(4):
            r = panel * WINDOW + 8 + d
            rows.append(lost[d] + cr[r : r + 1])
    rows.append(jnp.zeros((4, BLOCK), f32))
    out_ref[80:96, :] = jnp.concatenate(rows, 0)


def pair_tables(rank, pairs, weights):
    vmem = pl.BlockSpec(memory_space=pltpu.VMEM)
    return pl.pallas_call(
        tables_kernel,
        name="pair_tables",
        in_specs=[pl.BlockSpec(memory_space=pltpu.SMEM), vmem, vmem],
        out_shape=jax.ShapeDtypeStruct((TABLE_ROWS, BLOCK), f32),
        scratch_shapes=[pltpu.VMEM((BLOCK, 256), f32)],
        compiler_params=pltpu.CompilerParams(vmem_limit_bytes=VMEM_BYTES),
        cost_estimate=pl.CostEstimate(
            flops=2 * CONFIGS * BLOCK * 256, bytes_accessed=12 * CONFIGS, transcendentals=0
        ),
    )(rank, pairs, weights)


def hessian_block(first_row, first_col, own, partner, diagonal):
    row = iota((BLOCK, BLOCK), 0) + first_row
    col = iota((BLOCK, BLOCK), 1) + first_col
    own_offset, own_weight = own
    partner_offset, partner_weight = partner
    value = jnp.where(row + own_offset == col, -own_weight, f32(0.0))
    value = value + jnp.where(col + partner_offset == row, -partner_weight, f32(0.0))
    return value + jnp.where(row == col, diagonal, f32(0.0))


def lane_column(tile, at):
    return jnp.broadcast_to(tile[:, at : at + 1], (8, BLOCK))


def sublane_row(tile, at):
    return jnp.broadcast_to(tile[at : at + 1, :], (8, BLOCK))


HALF = 8


def factor_tiles(tiles, beside):
    tiles = list(tiles)
    count = len(tiles)
    sub = iota((8, BLOCK), 0)
    lane = iota((8, BLOCK), 1)
    for begin in range(0, count, HALF):
        end = begin + HALF
        cols = [lane_column(tiles[begin], 8 * begin + j) for j in range(8)]
        for k in range(begin, end):
            base = 8 * k
            inside = (lane >= base) & (lane < base + 8)
            eye = jnp.where(lane == sub + base, f32(1.0), f32(0.0))
            entry = {(i, j): sublane_row(cols[j], i) for j in range(8) for i in range(j, 8)}
            own = jnp.where(inside, eye, tiles[k])
            if k < len(beside):
                beside[k]()
            rest = range(k + 1, end)
            left = {t: [lane_column(tiles[t], base + j) for j in range(8)] for t in rest}
            if k + 1 < end:
                ahead = [lane_column(tiles[k + 1], base + 8 + m) for m in range(8)]
            new = {t: jnp.where(inside, f32(0.0), tiles[t]) for t in rest}
            inverse = []
            for j in range(8):
                scale = 1.0 / entry[j, j]
                inverse.append(scale)
                ratio = {i: entry[i, j] * scale for i in range(j + 1, 8)}
                for i in range(j + 1, 8):
                    for m in range(j + 1, i + 1):
                        entry[i, m] = entry[i, m] - ratio[i] * entry[m, j]
                row = sublane_row(own, j)
                if j < 7:
                    step = jnp.where(sub > j, cols[j] * scale, f32(0.0))
                    for m in range(j + 1, 8):
                        cols[m] = cols[m] - step * entry[m, j]
                    own = own - step * row
                for t in rest:
                    step = left[t][j] * scale
                    if t == k + 1:
                        for m in range(8):
                            ahead[m] = ahead[m] - step * sublane_row(left[t][j], m)
                    for m in range(j + 1, 8):
                        left[t][m] = left[t][m] - step * entry[m, j]
                    new[t] = new[t] - step * row
            for t in rest:
                tiles[t] = new[t]
            scale = inverse[0]
            for j in range(1, 8):
                scale = jnp.where(sub == j, inverse[j], scale)
            tiles[k] = own * jnp.sqrt(scale)
            if k + 1 < end:
                cols = ahead
        if end < count:
            rows = jnp.concatenate(tiles[begin:end], 0)
            wide_lane, wide_sub = iota(rows.shape, 1), iota(rows.shape, 0) + 8 * begin
            keep = (wide_lane <= wide_sub) | (wide_lane >= 8 * end)
            product = dot3(split2(rows.T[8 * end :, :]), split2(jnp.where(keep, rows, f32(0.0))))
            gone = (lane >= 8 * begin) & (lane < 8 * end)
            for n, t in enumerate(range(end, count)):
                tiles[t] = jnp.where(gone, f32(0.0), tiles[t]) - product[8 * n : 8 * n + 8, :]
    return tiles


def dot3(left, right):
    lh, ll = left
    rh, rl = right
    return dot_nn(lh, rh) + (dot_nn(lh, rl) + dot_nn(ll, rh))


def points_parts(value, scale):
    high, middle = split2(value * scale)
    return high, middle, high.astype(f32) + middle.astype(f32)


def chain_kernel(
    rank_ref, mine_ref, other_ref, inv_ref, feat_ref, factor_hbm, schur_hbm,
    x_ref, dg_ref, offc_ref, cc_ref, offr_ref, cr_ref, b4_ref, csq_ref, pts_ref, t_ref, lower_ref, d_ref,
    wh_ref, wl_ref, uh_ref, ul_ref, sh_ref, sl_ref, s2_ref, mh_ref, ml_ref, out_ref, out_sem,
):
    r_rank = rank_ref[0]
    c = rank_ref[1]
    even = (r_rank & 1) == 0
    scale = inv_ref[...] * ROOT_LOG2E

    def of_panel(panel, rows):
        return jnp.where(even == (panel != 1), mine_ref[rows, :], other_ref[rows, :])

    at = slice(4 * QUARTER, 4 * QUARTER + TABLE_ROWS)
    table = mine_ref[at, :] + other_ref[at, :]
    offr = table[0:40].astype(i32)
    cr = table[40:80]
    offr_ref[...] = offr
    cr_ref[...] = cr
    offc_ref[...] = jnp.concatenate([offr, jnp.zeros((88, BLOCK), i32)], 0).T
    cc_ref[...] = jnp.concatenate([cr, jnp.zeros((88, BLOCK), f32)], 0).T
    dg_ref[...] = table[80:96]
    for k in range(4):
        place = (c + k) & 3
        first = k * QUARTER
        for panel in range(2):
            rows = pl.ds(pl.multiple_of(panel * PANEL + place * BLOCK, BLOCK), BLOCK)
            pts_ref[rows, :] = of_panel(panel, slice(first, first + BLOCK))
            dg_ref[pl.ds(panel * 4 + place, 1), :] += of_panel(panel, slice(first + BLOCK, first + BLOCK + 1))
    first = 4 * QUARTER + TABLE_ROWS
    pts_ref[CHAIN:COLUMNS, :] = of_panel(2, slice(first, first + BLOCK))
    dg_ref[pl.ds(8 + c, 1), :] += of_panel(2, slice(first + BLOCK, first + BLOCK + 1))

    for k in range(9):
        cols = slice(k * BLOCK, (k + 1) * BLOCK)
        high, middle, near = points_parts(pts_ref[cols, :], scale)
        near = near.T
        csq_ref[:, cols] = jnp.broadcast_to(1.0 - 0.5 * jnp.sum(near * near, axis=0, keepdims=True), (8, BLOCK))
        high, middle = split2(near)
        for n, part in enumerate((high, middle, high, middle)):
            b4_ref[n * BLOCK : (n + 1) * BLOCK, cols] = part

    def kernel_rows(value, cols):
        high, middle, near = points_parts(value, scale)
        own_sq = -0.5 * jnp.sum(near * near, axis=1, keepdims=True)
        inner = dot_nn(jnp.concatenate([high, high, middle, middle], 1), b4_ref[:, cols])
        return jnp.exp2(inner + (own_sq + csq_ref[0:1, cols]))

    for k in range(8):
        rows = slice(k * BLOCK, (k + 1) * BLOCK)
        x_ref[rows, k * BLOCK :] = kernel_rows(pts_ref[rows, :], slice(k * BLOCK, COLUMNS))
        if k:
            x_ref[rows, : k * BLOCK] = jnp.zeros((BLOCK, k * BLOCK), f32)
    for ref in (wh_ref, wl_ref, uh_ref, ul_ref, t_ref, lower_ref):
        ref[...] = jnp.zeros_like(ref)
    for panel in range(2):
        for b in range(4):
            r = panel * WINDOW + 8 + b
            for d in range(b, 4):
                s = panel * WINDOW + 8 + d
                at = (
                    slice(panel * PANEL + b * BLOCK, panel * PANEL + (b + 1) * BLOCK),
                    slice(panel * PANEL + d * BLOCK, panel * PANEL + (d + 1) * BLOCK),
                )
                line = panel * 4 + d
                x_ref[at] += hessian_block(
                    b * BLOCK, d * BLOCK,
                    (offc_ref[:, r : r + 1], cc_ref[:, r : r + 1]),
                    (offr_ref[s : s + 1, :], cr_ref[s : s + 1, :]),
                    dg_ref[line : line + 1, :],
                )

    sub = iota((8, BLOCK), 0)
    lane = iota((8, BLOCK), 1)
    d_ref[...] = x_ref[:BLOCK, :BLOCK]

    def block_rows(index):
        return pl.ds(pl.multiple_of(index * BLOCK, BLOCK), BLOCK)

    def finish_row(k, depth, turn_from):
        own = block_rows(k)
        row = dot3(split2(lower_ref[...]), split2(t_ref[...]))
        high, low = split2(row)
        wh_ref[:depth, own] = jnp.zeros((depth, BLOCK), bf16)
        wl_ref[:depth, own] = jnp.zeros((depth, BLOCK), bf16)
        wh_ref[own, :] = high
        wl_ref[own, :] = low
        for i in range(turn_from, 8):
            turned_high, turned_low = split2(row[:, i * BLOCK : (i + 1) * BLOCK].T)
            uh_ref[i * BLOCK : (i + 1) * BLOCK, own] = turned_high
            ul_ref[i * BLOCK : (i + 1) * BLOCK, own] = turned_low

    def panel_step(k, depth, turn_from):
        own = block_rows(k)
        following = jnp.minimum(k + 1, 7)
        after = block_rows(following)
        spans = [slice(n, min(n + 256, COLUMNS)) for n in range(0, COLUMNS, 256)]

        rows = pl.ds(pl.multiple_of(k * ROW_STEP, ROW_STEP), ROW_STEP)
        high, middle, near = points_parts(feat_ref[rows, :], scale)
        own_sq = -0.5 * jnp.sum(near * near, axis=1, keepdims=True)
        parts = jnp.concatenate([high, high, middle, middle], 1)

        def entries(cols):
            value = jnp.exp2(dot_nn(parts, b4_ref[:, cols]) + (own_sq + csq_ref[0:1, cols]))
            if cols.start == CHAIN:
                s2_ref[rows, :] = value
            else:
                sh_ref[rows, cols], sl_ref[rows, cols] = split2(value)

        finish_row(jnp.maximum(k - 1, 0), depth, turn_from)
        left = (uh_ref[own, :depth], ul_ref[own, :depth])

        def row_part(cols):
            t_ref[:, cols] = x_ref[own, cols] - dot3(left, (wh_ref[:depth, cols], wl_ref[:depth, cols]))

        def identity_part():
            for t in range(16):
                t_ref[8 * t : 8 * t + 8, own] = jnp.where(lane == sub + 8 * t, f32(1.0), f32(0.0))

        block = []

        def next_block():
            other = (uh_ref[after, :depth], ul_ref[after, :depth])
            block.append(x_ref[after, after] - dot3(other, (wh_ref[:depth, after], wl_ref[:depth, after])))

        beside = [functools.partial(entries, cols) for cols in spans]
        beside += [functools.partial(row_part, cols) for cols in spans] + [identity_part, next_block]
        tiles = factor_tiles([d_ref[8 * t : 8 * t + 8, :] for t in range(16)], beside)

        lower = jnp.concatenate([jnp.where(lane <= sub + 8 * t, tiles[t], f32(0.0)) for t in range(16)], 0)
        lower_ref[...] = lower
        upper = dot3(split2(lower), split2(t_ref[:, after]))
        d_ref[...] = block[0] - dot3(split2(upper.T), split2(upper))

    def first_half(k, carry):
        panel_step(k, PANEL, 1)
        return carry

    def second_half(k, carry):
        panel_step(k, CHAIN, 4)
        return carry

    lax.fori_loop(0, 4, first_half, 0)
    lax.fori_loop(4, 8, second_half, 0)
    finish_row(7, CHAIN, 8)

    def add_hessian(panel, first_row, device_row, count, from_row, from_col):
        pick_lane = iota((BLOCK, BLOCK), 1)

        def added(value, start, first_col, offset, weight, diagonal):
            col = iota(value.shape, 1) + first_col
            if from_row:
                pick = pick_lane == panel * WINDOW + 8 + start // BLOCK
                target = jnp.sum(jnp.where(pick, offc_ref[...], 0), axis=1, keepdims=True)
                target = target + (iota((BLOCK, 1), 0) + start)
                own_weight = jnp.sum(jnp.where(pick, cc_ref[...], f32(0.0)), axis=1, keepdims=True)
                value = value - jnp.where(col == target, own_weight, f32(0.0))
            if from_col:
                row = iota(value.shape, 0) + start
                target = iota((1, value.shape[1]), 1) + (first_col + offset)
                value = value - jnp.where(row == target, weight, f32(0.0))
                if from_row:
                    value = value + jnp.where(row == col, diagonal, f32(0.0))
            return value

        def per_block(b, carry):
            start = first_row + b * BLOCK
            rows = block_rows(device_row // BLOCK + b)

            @pl.when(panel == 2)
            def _():
                at = pl.ds(2 * WINDOW + 8 + c, 1)
                s2_ref[rows, :] = added(
                    s2_ref[rows, :], start, c * BLOCK, offr_ref[at, :], cr_ref[at, :], dg_ref[pl.ds(8 + c, 1), :]
                )

            @pl.when(panel < 2)
            def _():
                cols = pl.ds(pl.multiple_of(panel * PANEL, PANEL), PANEL)
                lines = [panel * WINDOW + 8 + d for d in range(4)]
                offset = jnp.concatenate([offr_ref[pl.ds(line, 1), :] for line in lines], 1)
                weight = jnp.concatenate([cr_ref[pl.ds(line, 1), :] for line in lines], 1)
                diagonal = jnp.concatenate([dg_ref[pl.ds(panel * 4 + d, 1), :] for d in range(4)], 1)
                value = sh_ref[rows, cols].astype(f32) + sl_ref[rows, cols].astype(f32)
                high, low = split2(added(value, start, 0, offset, weight, diagonal))
                sh_ref[rows, cols] = high
                sl_ref[rows, cols] = low

            return carry

        lax.fori_loop(0, count, per_block, 0)

    @pl.when(r_rank <= 2)
    def _():
        add_hessian(r_rank, 0, 0, 4, True, True)
        add_hessian(r_rank, PANEL, PANEL, 8, False, True)

    next_panel = jnp.where(r_rank == 31, 0, r_rank + 1)

    @pl.when(next_panel <= 2)
    def _():
        add_hessian(next_panel, -1024, ROWS_DEV - 1024, 8, True, False)

    for panel in range(2):
        rows = pl.ds(pl.multiple_of(panel * PANEL + c * BLOCK, BLOCK), BLOCK)
        value = wh_ref[rows, :CHAIN].astype(f32) + wl_ref[rows, :CHAIN].astype(f32)
        for n in range(8):
            high, low = split2(value[:, n * BLOCK : (n + 1) * BLOCK].T)
            mh_ref[n * BLOCK : (n + 1) * BLOCK, panel * BLOCK : (panel + 1) * BLOCK] = high
            ml_ref[n * BLOCK : (n + 1) * BLOCK, panel * BLOCK : (panel + 1) * BLOCK] = low
    turned = jnp.concatenate(
        [
            (wh_ref[rows, CHAIN:].astype(f32) + wl_ref[rows, CHAIN:].astype(f32)).T
            for rows in (slice(i * BLOCK, (i + 1) * BLOCK) for i in range(8))
        ],
        1,
    )
    value = dot3(split2(turned), (wh_ref[:, :CHAIN], wl_ref[:, :CHAIN]))
    for n in range(8):
        high, low = split2(-value[:, n * BLOCK : (n + 1) * BLOCK].T)
        mh_ref[n * BLOCK : (n + 1) * BLOCK, 2 * BLOCK :] = high
        ml_ref[n * BLOCK : (n + 1) * BLOCK, 2 * BLOCK :] = low

    def copies(n):
        rows = pl.ds(pl.multiple_of(n * ROW_STEP, ROW_STEP), ROW_STEP)
        return [
            pltpu.make_async_copy(out_ref.at[0, rows], factor_hbm.at[0, rows], out_sem.at[n, 0]),
            pltpu.make_async_copy(out_ref.at[1, rows], factor_hbm.at[1, rows], out_sem.at[n, 1]),
            pltpu.make_async_copy(out_ref.at[2, rows], schur_hbm.at[rows], out_sem.at[n, 2]),
        ]

    def out_step(n, carry):
        rows = pl.ds(pl.multiple_of(n * ROW_STEP, ROW_STEP), ROW_STEP)
        both = (sh_ref[rows, :], sl_ref[rows, :])
        rest = dot3(both, (mh_ref[:, BLOCK:], ml_ref[:, BLOCK:]))
        both = (sh_ref[rows, :PANEL], sl_ref[rows, :PANEL])
        packed = jnp.concatenate([mh_ref[:PANEL, :BLOCK], ml_ref[:PANEL, :BLOCK]], 1)
        head = dot_nn(both[0], packed) + dot_nn(both[1], packed)
        head = head[:, :BLOCK] + head[:, BLOCK:]
        keep_second = jnp.where((r_rank == 0) & (n == 0), f32(0.0), f32(1.0))
        keep_schur = jnp.where((r_rank <= 1) & (n == 0), f32(0.0), f32(1.0))
        out_ref[0, rows, :] = head
        out_ref[1, rows, :] = rest[:, :BLOCK] * keep_second
        out_ref[2, rows, :] = (s2_ref[rows, :] + rest[:, BLOCK:]) * keep_schur
        for copy in copies(n):
            copy.start()
        return carry

    lax.fori_loop(0, ROW_STEPS, out_step, 0)
    for n in range(ROW_STEPS):
        for copy in copies(n):
            copy.wait()


def panel_chain(rank, mine, other, inv_length, features):
    vmem = pl.BlockSpec(memory_space=pltpu.VMEM)
    anywhere = pl.BlockSpec(memory_space=pl.ANY)
    return pl.pallas_call(
        chain_kernel,
        name="panel_chain",
        in_specs=[pl.BlockSpec(memory_space=pltpu.SMEM)] + [vmem] * 4,
        out_specs=(anywhere, anywhere),
        out_shape=(
            jax.ShapeDtypeStruct((2, ROWS_DEV, BLOCK), f32),
            jax.ShapeDtypeStruct((ROWS_DEV, BLOCK), f32),
        ),
        scratch_shapes=[
            pltpu.VMEM((CHAIN, COLUMNS), f32),
            pltpu.VMEM((16, BLOCK), f32),
            pltpu.VMEM((BLOCK, BLOCK), i32),
            pltpu.VMEM((BLOCK, BLOCK), f32),
            pltpu.VMEM((40, BLOCK), i32),
            pltpu.VMEM((40, BLOCK), f32),
            pltpu.VMEM((PANEL, COLUMNS), bf16),
            pltpu.VMEM((8, COLUMNS), f32),
            pltpu.VMEM((COLUMNS, BLOCK), f32),
            pltpu.VMEM((BLOCK, COLUMNS), f32),
            pltpu.VMEM((BLOCK, BLOCK), f32),
            pltpu.VMEM((BLOCK, BLOCK), f32),
            pltpu.VMEM((CHAIN, COLUMNS), bf16),
            pltpu.VMEM((CHAIN, COLUMNS), bf16),
            pltpu.VMEM((CHAIN, CHAIN), bf16),
            pltpu.VMEM((CHAIN, CHAIN), bf16),
            pltpu.VMEM((ROWS_DEV, CHAIN), bf16),
            pltpu.VMEM((ROWS_DEV, CHAIN), bf16),
            pltpu.VMEM((ROWS_DEV, BLOCK), f32),
            pltpu.VMEM((CHAIN, 3 * BLOCK), bf16),
            pltpu.VMEM((CHAIN, 3 * BLOCK), bf16),
            pltpu.VMEM((3, ROWS_DEV, BLOCK), f32),
            pltpu.SemaphoreType.DMA((ROW_STEPS, 3)),
        ],
        compiler_params=pltpu.CompilerParams(vmem_limit_bytes=VMEM_BYTES),
        cost_estimate=pl.CostEstimate(
            flops=6 * ROWS_DEV * COLUMNS * CHAIN, bytes_accessed=12 * 1024 * 1024, transcendentals=ROWS_DEV * COLUMNS
        ),
    )(rank, mine, other, inv_length, features)


def row_index(z, y, core):
    return (z % 4) * 8 + (y % 4) * 2 + core


def share_panels(features, nugget, tables):
    row = lax.axis_index("row")
    col = lax.axis_index("col")
    z, y = row // 8, (row // 2) % 4
    quarter = lax.dynamic_slice_in_dim(features, col * BLOCK, BLOCK, 0)
    extra = lax.dynamic_slice_in_dim(nugget, col * BLOCK, BLOCK, 0)[None, :]
    mine = jnp.concatenate([quarter, jnp.broadcast_to(extra, (8, BLOCK))], 0)

    def send(value, pairs):
        return lax.ppermute(value, "row", pairs)

    along_z = [
        send(mine, [(row_index(0, *at), row_index(k, *at)) for at in ((0, 0), (0, 1), (1, 0))]) for k in (1, 2, 3)
    ]
    for k in (1, 2, 3):
        mine = jnp.where(z == k, along_z[k - 1], mine)
    along_y = [
        send(
            mine,
            [
                (row_index(k, at, half), row_index(k, at + s, half))
                for k in range(4)
                for at, half in ((0, 0), (0, 1), (1, 0))
            ],
        )
        for s in (1, 2, 3)
    ]
    first, third = mine, mine
    for s in (1, 2, 3):
        first = jnp.where(y == s, along_y[s - 1], first)
        third = jnp.where(y == (1 + s) % 4, along_y[s - 1], third)
    part = jnp.concatenate([first, tables], 0)
    parts = [part] + [lax.ppermute(part, "col", [((i + k) % 4, i) for i in range(4)]) for k in (1, 2, 3)]
    summed = (parts[0][QUARTER:] + parts[1][QUARTER:]) + (parts[2][QUARTER:] + parts[3][QUARTER:])
    held = jnp.concatenate([part[:QUARTER] for part in parts] + [summed, third], 0)
    return held, send(held, [(i, i ^ 1) for i in range(32)])


def per_device(features, inv_length, nugget, pairs, weights):
    rank = jnp.stack([lax.axis_index("row"), lax.axis_index("col")]).astype(i32)
    tables = pair_tables(rank, pairs, weights.reshape(1, CONFIGS))
    mine, other = share_panels(features, nugget, tables)
    return panel_chain(rank, mine, other, inv_length.reshape(1, BLOCK), features)


def solution(mesh):
    placed = (P("row", None), P(), P("row"), P(), P())
    return jax.shard_map(
        per_device,
        mesh=mesh,
        in_specs=placed,
        out_specs=(P(None, "row", "col"), P("row", "col")),
        check_vma=False,
    )
```

```python
import functools

import jax
import jax.numpy as jnp
from jax import lax
from jax.experimental import pallas as pl
from jax.experimental.pallas import tpu as pltpu
from jax.sharding import PartitionSpec as P

PANEL = 512
ROWS_DEV = 4096
CONFIGS = 131072
BLOCK = 128
WINDOW = 12
CHAIN = 2 * PANEL
COLUMNS = CHAIN + BLOCK
ROW_STEP = 512
ROW_STEPS = ROWS_DEV // ROW_STEP
ROOT_LOG2E = 1.2011224087864498
VMEM_BYTES = 50 * 1024 * 1024
HIGHEST = lax.Precision.HIGHEST
f32, bf16, i32 = jnp.float32, jnp.bfloat16, jnp.int32


def iota(shape, dim):
    return lax.broadcasted_iota(i32, shape, dim)


def dot_nt(left, right, precision=None):
    return lax.dot_general(
        left, right, (((1,), (1,)), ((), ())), precision=precision, preferred_element_type=f32
    )


def dot_nn(left, right, precision=None):
    return lax.dot_general(
        left, right, (((1,), (0,)), ((), ())), precision=precision, preferred_element_type=f32
    )


def split3(value):
    high = value.astype(bf16)
    rest = value - high.astype(f32)
    middle = rest.astype(bf16)
    low = (rest - middle.astype(f32)).astype(bf16)
    return high, middle, low


def split2(value):
    high = value.astype(bf16)
    return high, (value - high.astype(f32)).astype(bf16)


TABLE_CHUNK = 4096
TABLE_ROWS = 96
TABLE_SHARE = CONFIGS // 8
QUARTER = BLOCK + 8


def tables_kernel(rank_ref, pairs_ref, weights_ref, out_ref, acc_ref):
    row = iota((40, 1), 0)
    code = row + 20 * ((row >= 12).astype(i32) + (row >= 24).astype(i32))
    code = jnp.where(row < 36, code, -1)
    low_id = iota((BLOCK, 1), 0)
    acc_ref[...] = jnp.zeros_like(acc_ref)

    def step(index, carry):
        span = pl.ds(pl.multiple_of(index * TABLE_CHUNK, TABLE_CHUNK), TABLE_CHUNK)
        winner = pairs_ref[0:1, span]
        loser = pairs_ref[1:2, span]
        weight = weights_ref[0:1, span]
        place = (winner + 1024) & (CONFIGS - 1)
        offset = (loser - winner) & (CONFIGS - 1)
        one_hot = jnp.where(low_id == (place & 127), f32(1.0), f32(0.0)).astype(bf16)
        hit = code == (place >> 7)
        parts = [(offset >> 5).astype(f32), (offset & 31).astype(f32)]
        parts += [part.astype(f32) for part in split3(weight)]
        values = [jnp.where(hit, part, f32(0.0)) for part in parts]
        values.append(jnp.zeros((8, TABLE_CHUNK), f32))
        acc_ref[...] += dot_nt(jnp.concatenate(values, 0).astype(bf16), one_hot)
        return carry

    lax.fori_loop(0, TABLE_SHARE // TABLE_CHUNK, step, 0)
    turned = acc_ref[...]
    offr = turned[0:40] * 32.0 + turned[40:80]
    cr = turned[80:120] + turned[120:160] + turned[160:200]
    out_ref[0:40, :] = offr
    out_ref[40:80, :] = cr
    offc = jnp.concatenate([offr.astype(i32), jnp.zeros((88, BLOCK), i32)], 0).T
    cc = jnp.concatenate([cr, jnp.zeros((88, BLOCK), f32)], 0).T
    place = iota((BLOCK, 1), 0)
    lane = iota((BLOCK, BLOCK), 1)
    rows = []
    for panel in range(3):
        lost = [jnp.zeros((1, BLOCK), f32) for _ in range(4)]
        for h in range(12):
            r = panel * WINDOW + h
            target = jnp.broadcast_to(offc[:, r : r + 1] + (place + BLOCK * (h - 8)), (BLOCK, BLOCK)) - lane
            weight = jnp.broadcast_to(cc[:, r : r + 1], (BLOCK, BLOCK))
            for d in range(4):
                if d <= h <= d + 8:
                    found = jnp.where(target == BLOCK * d, weight, f32(0.0))
                    lost[d] = lost[d] + jnp.sum(found, axis=0, keepdims=True)
        for d in range(4):
            r = panel * WINDOW + 8 + d
            rows.append(lost[d] + cr[r : r + 1])
    rows.append(jnp.zeros((4, BLOCK), f32))
    out_ref[80:96, :] = jnp.concatenate(rows, 0)


def pair_tables(rank, pairs, weights):
    def share(n, rank_ref):
        return 0, 2 * rank_ref[1] + (rank_ref[0] & 1)

    return pl.pallas_call(
        tables_kernel,
        name="pair_tables",
        grid_spec=pltpu.PrefetchScalarGridSpec(
            num_scalar_prefetch=1,
            grid=(1,),
            in_specs=[pl.BlockSpec((2, TABLE_SHARE), share), pl.BlockSpec((1, TABLE_SHARE), share)],
            out_specs=pl.BlockSpec((TABLE_ROWS, BLOCK), lambda n, rank_ref: (0, 0)),
            scratch_shapes=[pltpu.VMEM((208, BLOCK), f32)],
        ),
        out_shape=jax.ShapeDtypeStruct((TABLE_ROWS, BLOCK), f32),
        compiler_params=pltpu.CompilerParams(vmem_limit_bytes=VMEM_BYTES),
        cost_estimate=pl.CostEstimate(
            flops=2 * CONFIGS * BLOCK * 256, bytes_accessed=12 * CONFIGS, transcendentals=0
        ),
    )(rank, pairs, weights)


def lane_column(tile, at):
    return jnp.broadcast_to(tile[:, at : at + 1], (8, BLOCK))


def sublane_row(tile, at):
    return jnp.broadcast_to(tile[at : at + 1, :], (8, BLOCK))


HALF = 8


def factor_tiles(tiles, beside):
    tiles = list(tiles)
    count = len(tiles)
    sub = iota((8, BLOCK), 0)
    lane = iota((8, BLOCK), 1)
    for begin in range(0, count, HALF):
        end = begin + HALF
        cols = [lane_column(tiles[begin], 8 * begin + j) for j in range(8)]
        for k in range(begin, end):
            base = 8 * k
            inside = (lane >= base) & (lane < base + 8)
            eye = jnp.where(lane == sub + base, f32(1.0), f32(0.0))
            entry = {(i, j): sublane_row(cols[j], i) for j in range(8) for i in range(j, 8)}
            own = jnp.where(inside, eye, tiles[k])
            if k < len(beside):
                beside[k]()
            rest = range(k + 1, end)
            left = {t: [lane_column(tiles[t], base + j) for j in range(8)] for t in rest}
            if k + 1 < end:
                ahead = [lane_column(tiles[k + 1], base + 8 + m) for m in range(8)]
            new = {t: jnp.where(inside, f32(0.0), tiles[t]) for t in rest}
            inverse = []
            for j in range(8):
                scale = 1.0 / entry[j, j]
                inverse.append(scale)
                ratio = {i: entry[i, j] * scale for i in range(j + 1, 8)}
                for i in range(j + 1, 8):
                    for m in range(j + 1, i + 1):
                        entry[i, m] = entry[i, m] - ratio[i] * entry[m, j]
                row = sublane_row(own, j)
                if j < 7:
                    step = jnp.where(sub > j, cols[j] * scale, f32(0.0))
                    for m in range(j + 1, 8):
                        cols[m] = cols[m] - step * entry[m, j]
                    own = own - step * row
                for t in rest:
                    step = left[t][j] * scale
                    if t == k + 1:
                        for m in range(8):
                            ahead[m] = ahead[m] - step * sublane_row(left[t][j], m)
                    for m in range(j + 1, 8):
                        left[t][m] = left[t][m] - step * entry[m, j]
                    new[t] = new[t] - step * row
            for t in rest:
                tiles[t] = new[t]
            scale = inverse[0]
            for j in range(1, 8):
                scale = jnp.where(sub == j, inverse[j], scale)
            tiles[k] = own * jnp.sqrt(scale)
            if k + 1 < end:
                cols = ahead
        if end < count:
            rows = jnp.concatenate(tiles[begin:end], 0)
            wide_lane, wide_sub = iota(rows.shape, 1), iota(rows.shape, 0) + 8 * begin
            keep = (wide_lane <= wide_sub) | (wide_lane >= 8 * end)
            product = dot3(split2(rows.T[8 * end :, :]), split2(jnp.where(keep, rows, f32(0.0))))
            gone = (lane >= 8 * begin) & (lane < 8 * end)
            for n, t in enumerate(range(end, count)):
                tiles[t] = jnp.where(gone, f32(0.0), tiles[t]) - product[8 * n : 8 * n + 8, :]
    return tiles


def dot3(left, right):
    lh, ll = left
    rh, rl = right
    return dot_nn(lh, rh) + (dot_nn(lh, rl) + dot_nn(ll, rh))


def points_parts(value, scale):
    high, middle = split2(value * scale)
    return high, middle, high.astype(f32) + middle.astype(f32)


def chain_kernel(
    rank_ref, mine_ref, other_ref, inv_ref, feat_hbm, factor_hbm, schur_hbm,
    x_ref, dg_ref, offc_ref, cc_ref, offr_ref, cr_ref, b4_ref, csq_ref, pts_ref, t_ref, lower_ref, d_ref,
    wh_ref, wl_ref, uh_ref, ul_ref, sh_ref, sl_ref, s2_ref, mh_ref, ml_ref, out_ref, feat_ref, out_sem, feat_sem,
):
    r_rank = rank_ref[0]
    c = rank_ref[1]
    even = (r_rank & 1) == 0
    feat_copy = pltpu.make_async_copy(feat_hbm, feat_ref, feat_sem)
    feat_copy.start()
    scale = inv_ref[...] * ROOT_LOG2E

    def of_panel(panel, rows):
        return jnp.where(even == (panel != 1), mine_ref[rows, :], other_ref[rows, :])

    at = slice(4 * QUARTER, 4 * QUARTER + TABLE_ROWS)
    table = mine_ref[at, :] + other_ref[at, :]
    offr = table[0:40].astype(i32)
    cr = table[40:80]
    offr_ref[...] = offr
    cr_ref[...] = cr
    offc_ref[...] = jnp.concatenate([offr, jnp.zeros((88, BLOCK), i32)], 0).T
    cc_ref[...] = jnp.concatenate([cr, jnp.zeros((88, BLOCK), f32)], 0).T
    dg_ref[...] = table[80:96]
    for k in range(4):
        place = (c + k) & 3
        first = k * QUARTER
        for panel in range(2):
            rows = pl.ds(pl.multiple_of(panel * PANEL + place * BLOCK, BLOCK), BLOCK)
            pts_ref[rows, :] = of_panel(panel, slice(first, first + BLOCK))
            dg_ref[pl.ds(panel * 4 + place, 1), :] += of_panel(panel, slice(first + BLOCK, first + BLOCK + 1))
    first = 4 * QUARTER + TABLE_ROWS
    pts_ref[CHAIN:COLUMNS, :] = of_panel(2, slice(first, first + BLOCK))
    dg_ref[pl.ds(8 + c, 1), :] += of_panel(2, slice(first + BLOCK, first + BLOCK + 1))

    for k in range(9):
        cols = slice(k * BLOCK, (k + 1) * BLOCK)
        high, middle, near = points_parts(pts_ref[cols, :], scale)
        near = near.T
        csq_ref[:, cols] = jnp.broadcast_to(1.0 - 0.5 * jnp.sum(near * near, axis=0, keepdims=True), (8, BLOCK))
        high, middle = split2(near)
        for n, part in enumerate((high, middle, high, middle)):
            b4_ref[n * BLOCK : (n + 1) * BLOCK, cols] = part

    def kernel_rows(value, cols):
        high, middle, near = points_parts(value, scale)
        own_sq = -0.5 * jnp.sum(near * near, axis=1, keepdims=True)
        inner = dot_nn(jnp.concatenate([high, high, middle, middle], 1), b4_ref[:, cols])
        return jnp.exp2(inner + (own_sq + csq_ref[0:1, cols]))

    for ref in (wh_ref, wl_ref, uh_ref, ul_ref, t_ref, lower_ref):
        ref[...] = jnp.zeros_like(ref)
    sub = iota((8, BLOCK), 0)
    lane = iota((8, BLOCK), 1)

    def block_rows(index):
        return pl.ds(pl.multiple_of(index * BLOCK, BLOCK), BLOCK)

    def added(value, panel, start, first_col, lines, from_row, from_col):
        offset, weight, diagonal = lines
        col = iota(value.shape, 1) + first_col
        if from_row:
            pick = iota((BLOCK, BLOCK), 1) == panel * WINDOW + 8 + start // BLOCK
            target = jnp.sum(jnp.where(pick, offc_ref[...], 0), axis=1, keepdims=True)
            target = target + (iota((BLOCK, 1), 0) + start)
            own_weight = jnp.sum(jnp.where(pick, cc_ref[...], f32(0.0)), axis=1, keepdims=True)
            value = value - jnp.where(col == target, own_weight, f32(0.0))
        if from_col:
            row = iota(value.shape, 0) + start
            target = iota((1, value.shape[1]), 1) + (first_col + offset)
            value = value - jnp.where(row == target, weight, f32(0.0))
            if from_row:
                value = value + jnp.where(row == col, diagonal, f32(0.0))
        return value

    def panel_lines(panel):
        at = [pl.ds(panel * WINDOW + 8 + d, 1) for d in range(4)]
        return (
            jnp.concatenate([offr_ref[line, :] for line in at], 1),
            jnp.concatenate([cr_ref[line, :] for line in at], 1),
            jnp.concatenate([dg_ref[pl.ds(panel * 4 + d, 1), :] for d in range(4)], 1),
        )

    def system_row(i):
        rows = block_rows(i)
        value = kernel_rows(pts_ref[rows, :], slice(0, COLUMNS))
        x_ref[rows, :] = jnp.where(iota((BLOCK, COLUMNS), 1) >= i * BLOCK, value, f32(0.0))
        panel, start = i // 4, (i % 4) * BLOCK
        cols = pl.ds(pl.multiple_of(panel * PANEL, PANEL), PANEL)
        value = added(x_ref[rows, cols], panel, start, 0, panel_lines(panel), True, True)
        x_ref[rows, cols] = jnp.where(iota((BLOCK, PANEL), 1) >= start, value, f32(0.0))

    for i in range(8):
        system_row(i)
    d_ref[...] = x_ref[:BLOCK, :BLOCK]

    def finish_row(k, depth, turn_from):
        own = block_rows(k)
        row = dot3(split2(lower_ref[...]), split2(t_ref[...]))
        high, low = split2(row)
        wh_ref[:depth, own] = jnp.zeros((depth, BLOCK), bf16)
        wl_ref[:depth, own] = jnp.zeros((depth, BLOCK), bf16)
        wh_ref[own, :] = high
        wl_ref[own, :] = low
        for i in range(turn_from, 8):
            turned_high, turned_low = split2(row[:, i * BLOCK : (i + 1) * BLOCK].T)
            uh_ref[i * BLOCK : (i + 1) * BLOCK, own] = turned_high
            ul_ref[i * BLOCK : (i + 1) * BLOCK, own] = turned_low

    def panel_step(k, depth, turn_from):
        own = block_rows(k)
        following = jnp.minimum(k + 1, 7)
        after = block_rows(following)
        spans = [slice(n, min(n + 256, COLUMNS)) for n in range(0, COLUMNS, 256)]

        rows = pl.ds(pl.multiple_of(k * ROW_STEP, ROW_STEP), ROW_STEP)
        high, middle, near = points_parts(feat_ref[rows, :], scale)
        own_sq = -0.5 * jnp.sum(near * near, axis=1, keepdims=True)
        parts = jnp.concatenate([high, high, middle, middle], 1)

        def entries(cols):
            value = jnp.exp2(dot_nn(parts, b4_ref[:, cols]) + (own_sq + csq_ref[0:1, cols]))
            if cols.start == CHAIN:
                s2_ref[rows, :] = value
            else:
                sh_ref[rows, cols], sl_ref[rows, cols] = split2(value)

        finish_row(jnp.maximum(k - 1, 0), depth, turn_from)
        left = (uh_ref[own, :depth], ul_ref[own, :depth])

        def row_part(cols):
            t_ref[:, cols] = x_ref[own, cols] - dot3(left, (wh_ref[:depth, cols], wl_ref[:depth, cols]))

        def identity_part():
            for t in range(16):
                t_ref[8 * t : 8 * t + 8, own] = jnp.where(lane == sub + 8 * t, f32(1.0), f32(0.0))

        block = []

        def next_block():
            other = (uh_ref[after, :depth], ul_ref[after, :depth])
            block.append(x_ref[after, after] - dot3(other, (wh_ref[:depth, after], wl_ref[:depth, after])))

        beside = [functools.partial(entries, cols) for cols in spans]
        beside += [functools.partial(row_part, cols) for cols in spans] + [identity_part, next_block]
        tiles = factor_tiles([d_ref[8 * t : 8 * t + 8, :] for t in range(16)], beside)

        lower = jnp.concatenate([jnp.where(lane <= sub + 8 * t, tiles[t], f32(0.0)) for t in range(16)], 0)
        lower_ref[...] = lower
        upper = dot3(split2(lower), split2(t_ref[:, after]))
        d_ref[...] = block[0] - dot3(split2(upper.T), split2(upper))

    def first_half(k, carry):
        panel_step(k, PANEL, 1)
        return carry

    def second_half(k, carry):
        panel_step(k, CHAIN, 4)
        return carry

    feat_copy.wait()
    lax.fori_loop(0, 4, first_half, 0)
    lax.fori_loop(4, 8, second_half, 0)
    finish_row(7, CHAIN, 8)

    def add_hessian(panel, first_row, device_row, count, from_row, from_col):
        def per_block(b, carry):
            start = first_row + b * BLOCK
            rows = block_rows(device_row // BLOCK + b)

            @pl.when(panel == 2)
            def _():
                at = pl.ds(2 * WINDOW + 8 + c, 1)
                lines = (offr_ref[at, :], cr_ref[at, :], dg_ref[pl.ds(8 + c, 1), :])
                s2_ref[rows, :] = added(s2_ref[rows, :], panel, start, c * BLOCK, lines, from_row, from_col)

            @pl.when(panel < 2)
            def _():
                cols = pl.ds(pl.multiple_of(panel * PANEL, PANEL), PANEL)
                value = sh_ref[rows, cols].astype(f32) + sl_ref[rows, cols].astype(f32)
                high, low = split2(added(value, panel, start, 0, panel_lines(panel), from_row, from_col))
                sh_ref[rows, cols] = high
                sl_ref[rows, cols] = low

            return carry

        lax.fori_loop(0, count, per_block, 0)

    @pl.when(r_rank <= 2)
    def _():
        add_hessian(r_rank, 0, 0, 4, True, True)
        add_hessian(r_rank, PANEL, PANEL, 8, False, True)

    next_panel = jnp.where(r_rank == 31, 0, r_rank + 1)

    @pl.when(next_panel <= 2)
    def _():
        add_hessian(next_panel, -1024, ROWS_DEV - 1024, 8, True, False)

    for panel in range(2):
        rows = pl.ds(pl.multiple_of(panel * PANEL + c * BLOCK, BLOCK), BLOCK)
        value = wh_ref[rows, :CHAIN].astype(f32) + wl_ref[rows, :CHAIN].astype(f32)
        for n in range(8):
            high, low = split2(value[:, n * BLOCK : (n + 1) * BLOCK].T)
            mh_ref[n * BLOCK : (n + 1) * BLOCK, panel * BLOCK : (panel + 1) * BLOCK] = high
            ml_ref[n * BLOCK : (n + 1) * BLOCK, panel * BLOCK : (panel + 1) * BLOCK] = low
    turned = jnp.concatenate(
        [
            (wh_ref[rows, CHAIN:].astype(f32) + wl_ref[rows, CHAIN:].astype(f32)).T
            for rows in (slice(i * BLOCK, (i + 1) * BLOCK) for i in range(8))
        ],
        1,
    )
    value = dot3(split2(turned), (wh_ref[:, :CHAIN], wl_ref[:, :CHAIN]))
    for n in range(8):
        high, low = split2(-value[:, n * BLOCK : (n + 1) * BLOCK].T)
        mh_ref[n * BLOCK : (n + 1) * BLOCK, 2 * BLOCK :] = high
        ml_ref[n * BLOCK : (n + 1) * BLOCK, 2 * BLOCK :] = low

    def copies(n):
        rows = pl.ds(pl.multiple_of(n * ROW_STEP, ROW_STEP), ROW_STEP)
        return [
            pltpu.make_async_copy(out_ref.at[0, rows], factor_hbm.at[0, rows], out_sem.at[n, 0]),
            pltpu.make_async_copy(out_ref.at[1, rows], factor_hbm.at[1, rows], out_sem.at[n, 1]),
            pltpu.make_async_copy(out_ref.at[2, rows], schur_hbm.at[rows], out_sem.at[n, 2]),
        ]

    def out_step(n, carry):
        rows = pl.ds(pl.multiple_of(n * ROW_STEP, ROW_STEP), ROW_STEP)
        both = (sh_ref[rows, :], sl_ref[rows, :])
        rest = dot3(both, (mh_ref[:, BLOCK:], ml_ref[:, BLOCK:]))
        both = (sh_ref[rows, :PANEL], sl_ref[rows, :PANEL])
        packed = jnp.concatenate([mh_ref[:PANEL, :BLOCK], ml_ref[:PANEL, :BLOCK]], 1)
        head = dot_nn(both[0], packed) + dot_nn(both[1], packed)
        head = head[:, :BLOCK] + head[:, BLOCK:]
        keep_second = jnp.where((r_rank == 0) & (n == 0), f32(0.0), f32(1.0))
        keep_schur = jnp.where((r_rank <= 1) & (n == 0), f32(0.0), f32(1.0))
        out_ref[0, rows, :] = head
        out_ref[1, rows, :] = rest[:, :BLOCK] * keep_second
        out_ref[2, rows, :] = (s2_ref[rows, :] + rest[:, BLOCK:]) * keep_schur
        for copy in copies(n):
            copy.start()
        return carry

    lax.fori_loop(0, ROW_STEPS, out_step, 0)
    for n in range(ROW_STEPS):
        for copy in copies(n):
            copy.wait()


def panel_chain(rank, mine, other, inv_length, features):
    vmem = pl.BlockSpec(memory_space=pltpu.VMEM)
    anywhere = pl.BlockSpec(memory_space=pl.ANY)
    return pl.pallas_call(
        chain_kernel,
        name="panel_chain",
        in_specs=[pl.BlockSpec(memory_space=pltpu.SMEM)] + [vmem] * 3 + [anywhere],
        out_specs=(anywhere, anywhere),
        out_shape=(
            jax.ShapeDtypeStruct((2, ROWS_DEV, BLOCK), f32),
            jax.ShapeDtypeStruct((ROWS_DEV, BLOCK), f32),
        ),
        scratch_shapes=[
            pltpu.VMEM((CHAIN, COLUMNS), f32),
            pltpu.VMEM((16, BLOCK), f32),
            pltpu.VMEM((BLOCK, BLOCK), i32),
            pltpu.VMEM((BLOCK, BLOCK), f32),
            pltpu.VMEM((40, BLOCK), i32),
            pltpu.VMEM((40, BLOCK), f32),
            pltpu.VMEM((PANEL, COLUMNS), bf16),
            pltpu.VMEM((8, COLUMNS), f32),
            pltpu.VMEM((COLUMNS, BLOCK), f32),
            pltpu.VMEM((BLOCK, COLUMNS), f32),
            pltpu.VMEM((BLOCK, BLOCK), f32),
            pltpu.VMEM((BLOCK, BLOCK), f32),
            pltpu.VMEM((CHAIN, COLUMNS), bf16),
            pltpu.VMEM((CHAIN, COLUMNS), bf16),
            pltpu.VMEM((CHAIN, CHAIN), bf16),
            pltpu.VMEM((CHAIN, CHAIN), bf16),
            pltpu.VMEM((ROWS_DEV, CHAIN), bf16),
            pltpu.VMEM((ROWS_DEV, CHAIN), bf16),
            pltpu.VMEM((ROWS_DEV, BLOCK), f32),
            pltpu.VMEM((CHAIN, 3 * BLOCK), bf16),
            pltpu.VMEM((CHAIN, 3 * BLOCK), bf16),
            pltpu.VMEM((3, ROWS_DEV, BLOCK), f32),
            pltpu.VMEM((ROWS_DEV, BLOCK), f32),
            pltpu.SemaphoreType.DMA((ROW_STEPS, 3)),
            pltpu.SemaphoreType.DMA,
        ],
        compiler_params=pltpu.CompilerParams(vmem_limit_bytes=VMEM_BYTES),
        cost_estimate=pl.CostEstimate(
            flops=6 * ROWS_DEV * COLUMNS * CHAIN, bytes_accessed=12 * 1024 * 1024, transcendentals=ROWS_DEV * COLUMNS
        ),
    )(rank, mine, other, inv_length, features)


def row_index(z, y, core):
    return (z % 4) * 8 + (y % 4) * 2 + core


def share_panels(features, nugget, tables):
    row = lax.axis_index("row")
    col = lax.axis_index("col")
    z, y = row // 8, (row // 2) % 4
    quarter = lax.dynamic_slice_in_dim(features, col * BLOCK, BLOCK, 0)
    extra = lax.dynamic_slice_in_dim(nugget.reshape(ROWS_DEV // BLOCK, BLOCK), col, 1, 0)
    mine = jnp.concatenate([quarter, jnp.broadcast_to(extra, (8, BLOCK))], 0)

    def send(value, pairs):
        return lax.ppermute(value, "row", pairs)

    along_z = [
        send(mine, [(row_index(0, *at), row_index(k, *at)) for at in ((0, 0), (0, 1), (1, 0))]) for k in (1, 2, 3)
    ]
    for k in (1, 2, 3):
        mine = jnp.where(z == k, along_z[k - 1], mine)
    along_y = [
        send(
            mine,
            [
                (row_index(k, at, half), row_index(k, at + s, half))
                for k in range(4)
                for at, half in ((0, 0), (0, 1), (1, 0))
            ],
        )
        for s in (1, 2, 3)
    ]
    first, third = mine, mine
    for s in (1, 2, 3):
        first = jnp.where(y == s, along_y[s - 1], first)
        third = jnp.where(y == (1 + s) % 4, along_y[s - 1], third)
    part = jnp.concatenate([first, tables], 0)
    parts = [part] + [lax.ppermute(part, "col", [((i + k) % 4, i) for i in range(4)]) for k in (1, 2, 3)]
    summed = (parts[0][QUARTER:] + parts[1][QUARTER:]) + (parts[2][QUARTER:] + parts[3][QUARTER:])
    held = jnp.concatenate([part[:QUARTER] for part in parts] + [summed, third], 0)
    return held, send(held, [(i, i ^ 1) for i in range(32)])


def per_device(features, inv_length, nugget, pairs, weights):
    rank = jnp.stack([lax.axis_index("row"), lax.axis_index("col")]).astype(i32)
    tables = pair_tables(rank, pairs, weights.reshape(1, CONFIGS))
    mine, other = share_panels(features, nugget, tables)
    return panel_chain(rank, mine, other, inv_length.reshape(1, BLOCK), features)


def solution(mesh):
    placed = (P("row", None), P(), P("row"), P(), P())
    return jax.shard_map(
        per_device,
        mesh=mesh,
        in_specs=placed,
        out_specs=(P(None, "row", "col"), P("row", "col")),
        check_vma=False,
    )
```

```python
import functools

import jax
import jax.numpy as jnp
from jax import lax
from jax.experimental import pallas as pl
from jax.experimental.pallas import tpu as pltpu
from jax.sharding import PartitionSpec as P

PANEL = 512
ROWS_DEV = 4096
CONFIGS = 131072
BLOCK = 128
WINDOW = 12
CHAIN = 2 * PANEL
COLUMNS = CHAIN + BLOCK
ROW_STEP = 512
ROW_STEPS = ROWS_DEV // ROW_STEP
ROOT_LOG2E = 1.2011224087864498
VMEM_BYTES = 50 * 1024 * 1024
HIGHEST = lax.Precision.HIGHEST
f32, bf16, i32 = jnp.float32, jnp.bfloat16, jnp.int32


def iota(shape, dim):
    return lax.broadcasted_iota(i32, shape, dim)


def dot_nt(left, right, precision=None):
    return lax.dot_general(
        left, right, (((1,), (1,)), ((), ())), precision=precision, preferred_element_type=f32
    )


def dot_nn(left, right, precision=None):
    return lax.dot_general(
        left, right, (((1,), (0,)), ((), ())), precision=precision, preferred_element_type=f32
    )


def split3(value):
    high = value.astype(bf16)
    rest = value - high.astype(f32)
    middle = rest.astype(bf16)
    low = (rest - middle.astype(f32)).astype(bf16)
    return high, middle, low


def split2(value):
    high = value.astype(bf16)
    return high, (value - high.astype(f32)).astype(bf16)


TABLE_CHUNK = 8192
TABLE_ROWS = 96
TABLE_SHARE = CONFIGS // 8
QUARTER = BLOCK + 8


def tables_kernel(rank_ref, pairs_ref, weights_ref, out_ref, acc_ref):
    row = iota((40, 1), 0)
    code = row + 20 * ((row >= 12).astype(i32) + (row >= 24).astype(i32))
    code = jnp.where(row < 36, code, -1)
    low_id = iota((BLOCK, 1), 0)
    acc_ref[...] = jnp.zeros_like(acc_ref)

    def step(index, carry):
        span = pl.ds(pl.multiple_of(index * TABLE_CHUNK, TABLE_CHUNK), TABLE_CHUNK)
        winner = pairs_ref[0:1, span]
        loser = pairs_ref[1:2, span]
        weight = weights_ref[0:1, span]
        place = (winner + 1024) & (CONFIGS - 1)
        offset = (loser - winner) & (CONFIGS - 1)
        one_hot = jnp.where(low_id == (place & 127), f32(1.0), f32(0.0)).astype(bf16)
        hit = code == (place >> 7)
        parts = [(offset >> 5).astype(f32), (offset & 31).astype(f32)]
        parts += [part.astype(f32) for part in split2(weight)]
        values = [jnp.where(hit, part, f32(0.0)) for part in parts]
        acc_ref[...] += dot_nt(jnp.concatenate(values, 0).astype(bf16), one_hot)
        return carry

    lax.fori_loop(0, TABLE_SHARE // TABLE_CHUNK, step, 0)
    turned = acc_ref[...]
    offr = turned[0:40] * 32.0 + turned[40:80]
    cr = turned[80:120] + turned[120:160]
    out_ref[0:40, :] = offr
    out_ref[40:80, :] = cr
    offc = jnp.concatenate([offr.astype(i32), jnp.zeros((88, BLOCK), i32)], 0).T
    cc = jnp.concatenate([cr, jnp.zeros((88, BLOCK), f32)], 0).T
    place = iota((BLOCK, 1), 0)
    lane = iota((BLOCK, BLOCK), 1)
    rows = []
    for panel in range(3):
        lost = [jnp.zeros((1, BLOCK), f32) for _ in range(4)]
        for h in range(12):
            r = panel * WINDOW + h
            target = jnp.broadcast_to(offc[:, r : r + 1] + (place + BLOCK * (h - 8)), (BLOCK, BLOCK)) - lane
            weight = jnp.broadcast_to(cc[:, r : r + 1], (BLOCK, BLOCK))
            for d in range(4):
                if d <= h <= d + 8:
                    found = jnp.where(target == BLOCK * d, weight, f32(0.0))
                    lost[d] = lost[d] + jnp.sum(found, axis=0, keepdims=True)
        for d in range(4):
            r = panel * WINDOW + 8 + d
            rows.append(lost[d] + cr[r : r + 1])
    rows.append(jnp.zeros((4, BLOCK), f32))
    out_ref[80:96, :] = jnp.concatenate(rows, 0)


def pair_tables(rank, pairs, weights):
    def share(n, rank_ref):
        return 0, 2 * rank_ref[1] + (rank_ref[0] & 1)

    return pl.pallas_call(
        tables_kernel,
        name="pair_tables",
        grid_spec=pltpu.PrefetchScalarGridSpec(
            num_scalar_prefetch=1,
            grid=(1,),
            in_specs=[pl.BlockSpec((2, TABLE_SHARE), share), pl.BlockSpec((1, TABLE_SHARE), share)],
            out_specs=pl.BlockSpec((TABLE_ROWS, BLOCK), lambda n, rank_ref: (0, 0)),
            scratch_shapes=[pltpu.VMEM((160, BLOCK), f32)],
        ),
        out_shape=jax.ShapeDtypeStruct((TABLE_ROWS, BLOCK), f32),
        compiler_params=pltpu.CompilerParams(vmem_limit_bytes=VMEM_BYTES),
        cost_estimate=pl.CostEstimate(
            flops=2 * CONFIGS * BLOCK * 256, bytes_accessed=12 * CONFIGS, transcendentals=0
        ),
    )(rank, pairs, weights)


def lane_column(tile, at):
    return jnp.broadcast_to(tile[:, at : at + 1], (8, BLOCK))


def sublane_row(tile, at):
    return jnp.broadcast_to(tile[at : at + 1, :], (8, BLOCK))


HALF = 8


def factor_tiles(tiles, beside):
    tiles = list(tiles)
    count = len(tiles)
    sub = iota((8, BLOCK), 0)
    lane = iota((8, BLOCK), 1)
    for begin in range(0, count, HALF):
        end = begin + HALF
        cols = [lane_column(tiles[begin], 8 * begin + j) for j in range(8)]
        for k in range(begin, end):
            base = 8 * k
            inside = (lane >= base) & (lane < base + 8)
            eye = jnp.where(lane == sub + base, f32(1.0), f32(0.0))
            entry = {(i, j): sublane_row(cols[j], i) for j in range(8) for i in range(j, 8)}
            own = jnp.where(inside, eye, tiles[k])
            if k < len(beside):
                beside[k]()
            rest = range(k + 1, end)
            left = {t: [lane_column(tiles[t], base + j) for j in range(8)] for t in rest}
            if k + 1 < end:
                ahead = [lane_column(tiles[k + 1], base + 8 + m) for m in range(8)]
            new = {t: jnp.where(inside, f32(0.0), tiles[t]) for t in rest}
            inverse = []
            for j in range(8):
                scale = 1.0 / entry[j, j]
                inverse.append(scale)
                ratio = {i: entry[i, j] * scale for i in range(j + 1, 8)}
                for i in range(j + 1, 8):
                    for m in range(j + 1, i + 1):
                        entry[i, m] = entry[i, m] - ratio[i] * entry[m, j]
                row = sublane_row(own, j)
                if j < 7:
                    step = jnp.where(sub > j, cols[j] * scale, f32(0.0))
                    for m in range(j + 1, 8):
                        cols[m] = cols[m] - step * entry[m, j]
                    own = own - step * row
                for t in rest:
                    step = left[t][j] * scale
                    if t == k + 1:
                        for m in range(8):
                            ahead[m] = ahead[m] - step * sublane_row(left[t][j], m)
                    for m in range(j + 1, 8):
                        left[t][m] = left[t][m] - step * entry[m, j]
                    new[t] = new[t] - step * row
            for t in rest:
                tiles[t] = new[t]
            scale = inverse[0]
            for j in range(1, 8):
                scale = jnp.where(sub == j, inverse[j], scale)
            tiles[k] = own * jnp.sqrt(scale)
            if k + 1 < end:
                cols = ahead
        if end < count:
            rows = jnp.concatenate(tiles[begin:end], 0)
            wide_lane, wide_sub = iota(rows.shape, 1), iota(rows.shape, 0) + 8 * begin
            keep = (wide_lane <= wide_sub) | (wide_lane >= 8 * end)
            product = dot3(split2(rows.T[8 * end :, :]), split2(jnp.where(keep, rows, f32(0.0))))
            gone = (lane >= 8 * begin) & (lane < 8 * end)
            for n, t in enumerate(range(end, count)):
                tiles[t] = jnp.where(gone, f32(0.0), tiles[t]) - product[8 * n : 8 * n + 8, :]
    return tiles


def dot3(left, right):
    lh, ll = left
    rh, rl = right
    return dot_nn(lh, rh) + (dot_nn(lh, rl) + dot_nn(ll, rh))


def points_parts(value, scale):
    high, middle = split2(value * scale)
    return high, middle, high.astype(f32) + middle.astype(f32)


def chain_kernel(
    rank_ref, mine_ref, other_ref, inv_ref, feat_hbm, factor_hbm, schur_hbm,
    x_ref, dg_ref, offc_ref, cc_ref, offr_ref, cr_ref, b4_ref, csq_ref, pts_ref, t_ref, lower_ref, d_ref,
    wh_ref, wl_ref, uh_ref, ul_ref, sh_ref, sl_ref, s2_ref, mh_ref, ml_ref, out_ref, feat_ref, out_sem, feat_sem,
):
    r_rank = rank_ref[0]
    c = rank_ref[1]
    even = (r_rank & 1) == 0
    feat_copy = pltpu.make_async_copy(feat_hbm, feat_ref, feat_sem)
    feat_copy.start()
    scale = inv_ref[...] * ROOT_LOG2E

    def of_panel(panel, rows):
        return jnp.where(even == (panel != 1), mine_ref[rows, :], other_ref[rows, :])

    at = slice(4 * QUARTER, 4 * QUARTER + TABLE_ROWS)
    table = mine_ref[at, :] + other_ref[at, :]
    offr = table[0:40].astype(i32)
    cr = table[40:80]
    offr_ref[...] = offr
    cr_ref[...] = cr
    offc_ref[...] = jnp.concatenate([offr, jnp.zeros((88, BLOCK), i32)], 0).T
    cc_ref[...] = jnp.concatenate([cr, jnp.zeros((88, BLOCK), f32)], 0).T
    dg_ref[...] = table[80:96]
    for k in range(4):
        place = (c + k) & 3
        first = k * QUARTER
        for panel in range(2):
            rows = pl.ds(pl.multiple_of(panel * PANEL + place * BLOCK, BLOCK), BLOCK)
            pts_ref[rows, :] = of_panel(panel, slice(first, first + BLOCK))
            dg_ref[pl.ds(panel * 4 + place, 1), :] += of_panel(panel, slice(first + BLOCK, first + BLOCK + 1))
    first = 4 * QUARTER + TABLE_ROWS
    pts_ref[CHAIN:COLUMNS, :] = of_panel(2, slice(first, first + BLOCK))
    dg_ref[pl.ds(8 + c, 1), :] += of_panel(2, slice(first + BLOCK, first + BLOCK + 1))

    for k in range(9):
        cols = slice(k * BLOCK, (k + 1) * BLOCK)
        high, middle, near = points_parts(pts_ref[cols, :], scale)
        near = near.T
        csq_ref[:, cols] = jnp.broadcast_to(1.0 - 0.5 * jnp.sum(near * near, axis=0, keepdims=True), (8, BLOCK))
        high, middle = split2(near)
        for n, part in enumerate((high, middle, high, middle)):
            b4_ref[n * BLOCK : (n + 1) * BLOCK, cols] = part

    def kernel_rows(value, cols):
        high, middle, near = points_parts(value, scale)
        own_sq = -0.5 * jnp.sum(near * near, axis=1, keepdims=True)
        inner = dot_nn(jnp.concatenate([high, high, middle, middle], 1), b4_ref[:, cols])
        return jnp.exp2(inner + (own_sq + csq_ref[0:1, cols]))

    for ref in (wh_ref, wl_ref, uh_ref, ul_ref, t_ref, lower_ref):
        ref[...] = jnp.zeros_like(ref)
    sub = iota((8, BLOCK), 0)
    lane = iota((8, BLOCK), 1)

    def block_rows(index):
        return pl.ds(pl.multiple_of(index * BLOCK, BLOCK), BLOCK)

    def added(value, panel, start, first_col, lines, from_row, from_col):
        offset, weight, diagonal = lines
        col = iota(value.shape, 1) + first_col
        if from_row:
            pick = iota((BLOCK, BLOCK), 1) == panel * WINDOW + 8 + start // BLOCK
            target = jnp.sum(jnp.where(pick, offc_ref[...], 0), axis=1, keepdims=True)
            target = target + (iota((BLOCK, 1), 0) + start)
            own_weight = jnp.sum(jnp.where(pick, cc_ref[...], f32(0.0)), axis=1, keepdims=True)
            value = value - jnp.where(col == target, own_weight, f32(0.0))
        if from_col:
            row = iota(value.shape, 0) + start
            target = iota((1, value.shape[1]), 1) + (first_col + offset)
            value = value - jnp.where(row == target, weight, f32(0.0))
            if from_row:
                value = value + jnp.where(row == col, diagonal, f32(0.0))
        return value

    def panel_lines(panel):
        at = [pl.ds(panel * WINDOW + 8 + d, 1) for d in range(4)]
        return (
            jnp.concatenate([offr_ref[line, :] for line in at], 1),
            jnp.concatenate([cr_ref[line, :] for line in at], 1),
            jnp.concatenate([dg_ref[pl.ds(panel * 4 + d, 1), :] for d in range(4)], 1),
        )

    def system_row(i):
        rows = block_rows(i)
        value = kernel_rows(pts_ref[rows, :], slice(0, COLUMNS))
        x_ref[rows, :] = jnp.where(iota((BLOCK, COLUMNS), 1) >= i * BLOCK, value, f32(0.0))
        panel, start = i // 4, (i % 4) * BLOCK
        cols = pl.ds(pl.multiple_of(panel * PANEL, PANEL), PANEL)
        value = added(x_ref[rows, cols], panel, start, 0, panel_lines(panel), True, True)
        x_ref[rows, cols] = jnp.where(iota((BLOCK, PANEL), 1) >= start, value, f32(0.0))

    for i in range(8):
        system_row(i)
    d_ref[...] = x_ref[:BLOCK, :BLOCK]

    def finish_row(k, depth, turn_from):
        own = block_rows(k)
        row = dot3(split2(lower_ref[...]), split2(t_ref[...]))
        high, low = split2(row)
        wh_ref[:depth, own] = jnp.zeros((depth, BLOCK), bf16)
        wl_ref[:depth, own] = jnp.zeros((depth, BLOCK), bf16)
        wh_ref[own, :] = high
        wl_ref[own, :] = low
        for i in range(turn_from, 8):
            turned_high, turned_low = split2(row[:, i * BLOCK : (i + 1) * BLOCK].T)
            uh_ref[i * BLOCK : (i + 1) * BLOCK, own] = turned_high
            ul_ref[i * BLOCK : (i + 1) * BLOCK, own] = turned_low

    def panel_step(k, depth, turn_from):
        own = block_rows(k)
        following = jnp.minimum(k + 1, 7)
        after = block_rows(following)
        spans = [slice(n, min(n + 256, COLUMNS)) for n in range(0, COLUMNS, 256)]

        rows = pl.ds(pl.multiple_of(k * ROW_STEP, ROW_STEP), ROW_STEP)
        high, middle, near = points_parts(feat_ref[rows, :], scale)
        own_sq = -0.5 * jnp.sum(near * near, axis=1, keepdims=True)
        parts = jnp.concatenate([high, high, middle, middle], 1)

        def entries(cols):
            value = jnp.exp2(dot_nn(parts, b4_ref[:, cols]) + (own_sq + csq_ref[0:1, cols]))
            if cols.start == CHAIN:
                s2_ref[rows, :] = value
            else:
                sh_ref[rows, cols], sl_ref[rows, cols] = split2(value)

        finish_row(jnp.maximum(k - 1, 0), depth, turn_from)
        left = (uh_ref[own, :depth], ul_ref[own, :depth])

        def row_part(cols):
            t_ref[:, cols] = x_ref[own, cols] - dot3(left, (wh_ref[:depth, cols], wl_ref[:depth, cols]))

        def identity_part():
            for t in range(16):
                t_ref[8 * t : 8 * t + 8, own] = jnp.where(lane == sub + 8 * t, f32(1.0), f32(0.0))

        block = []

        def next_block():
            other = (uh_ref[after, :depth], ul_ref[after, :depth])
            block.append(x_ref[after, after] - dot3(other, (wh_ref[:depth, after], wl_ref[:depth, after])))

        beside = [functools.partial(entries, cols) for cols in spans]
        beside += [functools.partial(row_part, cols) for cols in spans] + [identity_part, next_block]
        tiles = factor_tiles([d_ref[8 * t : 8 * t + 8, :] for t in range(16)], beside)

        lower = jnp.concatenate([jnp.where(lane <= sub + 8 * t, tiles[t], f32(0.0)) for t in range(16)], 0)
        lower_ref[...] = lower
        upper = dot3(split2(lower), split2(t_ref[:, after]))
        d_ref[...] = block[0] - dot3(split2(upper.T), split2(upper))

    def first_half(k, carry):
        panel_step(k, PANEL, 1)
        return carry

    def second_half(k, carry):
        panel_step(k, CHAIN, 4)
        return carry

    feat_copy.wait()
    lax.fori_loop(0, 4, first_half, 0)
    lax.fori_loop(4, 8, second_half, 0)
    finish_row(7, CHAIN, 8)

    def add_hessian(panel, first_row, device_row, count, from_row, from_col):
        def per_block(b, carry):
            start = first_row + b * BLOCK
            rows = block_rows(device_row // BLOCK + b)

            @pl.when(panel == 2)
            def _():
                at = pl.ds(2 * WINDOW + 8 + c, 1)
                lines = (offr_ref[at, :], cr_ref[at, :], dg_ref[pl.ds(8 + c, 1), :])
                s2_ref[rows, :] = added(s2_ref[rows, :], panel, start, c * BLOCK, lines, from_row, from_col)

            @pl.when(panel < 2)
            def _():
                cols = pl.ds(pl.multiple_of(panel * PANEL, PANEL), PANEL)
                value = sh_ref[rows, cols].astype(f32) + sl_ref[rows, cols].astype(f32)
                high, low = split2(added(value, panel, start, 0, panel_lines(panel), from_row, from_col))
                sh_ref[rows, cols] = high
                sl_ref[rows, cols] = low

            return carry

        lax.fori_loop(0, count, per_block, 0)

    @pl.when(r_rank <= 2)
    def _():
        add_hessian(r_rank, 0, 0, 4, True, True)
        add_hessian(r_rank, PANEL, PANEL, 8, False, True)

    next_panel = jnp.where(r_rank == 31, 0, r_rank + 1)

    @pl.when(next_panel <= 2)
    def _():
        add_hessian(next_panel, -1024, ROWS_DEV - 1024, 8, True, False)

    for panel in range(2):
        rows = pl.ds(pl.multiple_of(panel * PANEL + c * BLOCK, BLOCK), BLOCK)
        value = wh_ref[rows, :CHAIN].astype(f32) + wl_ref[rows, :CHAIN].astype(f32)
        for n in range(8):
            high, low = split2(value[:, n * BLOCK : (n + 1) * BLOCK].T)
            mh_ref[n * BLOCK : (n + 1) * BLOCK, panel * BLOCK : (panel + 1) * BLOCK] = high
            ml_ref[n * BLOCK : (n + 1) * BLOCK, panel * BLOCK : (panel + 1) * BLOCK] = low
    turned = jnp.concatenate(
        [
            (wh_ref[rows, CHAIN:].astype(f32) + wl_ref[rows, CHAIN:].astype(f32)).T
            for rows in (slice(i * BLOCK, (i + 1) * BLOCK) for i in range(8))
        ],
        1,
    )
    value = dot3(split2(turned), (wh_ref[:, :CHAIN], wl_ref[:, :CHAIN]))
    for n in range(8):
        high, low = split2(-value[:, n * BLOCK : (n + 1) * BLOCK].T)
        mh_ref[n * BLOCK : (n + 1) * BLOCK, 2 * BLOCK :] = high
        ml_ref[n * BLOCK : (n + 1) * BLOCK, 2 * BLOCK :] = low

    def copies(n):
        rows = pl.ds(pl.multiple_of(n * ROW_STEP, ROW_STEP), ROW_STEP)
        return [
            pltpu.make_async_copy(out_ref.at[0, rows], factor_hbm.at[0, rows], out_sem.at[n, 0]),
            pltpu.make_async_copy(out_ref.at[1, rows], factor_hbm.at[1, rows], out_sem.at[n, 1]),
            pltpu.make_async_copy(out_ref.at[2, rows], schur_hbm.at[rows], out_sem.at[n, 2]),
        ]

    def out_step(n, carry):
        rows = pl.ds(pl.multiple_of(n * ROW_STEP, ROW_STEP), ROW_STEP)
        both = (sh_ref[rows, :], sl_ref[rows, :])
        rest = dot3(both, (mh_ref[:, BLOCK:], ml_ref[:, BLOCK:]))
        both = (sh_ref[rows, :PANEL], sl_ref[rows, :PANEL])
        packed = jnp.concatenate([mh_ref[:PANEL, :BLOCK], ml_ref[:PANEL, :BLOCK]], 1)
        head = dot_nn(both[0], packed) + dot_nn(both[1], packed)
        head = head[:, :BLOCK] + head[:, BLOCK:]
        keep_second = jnp.where((r_rank == 0) & (n == 0), f32(0.0), f32(1.0))
        keep_schur = jnp.where((r_rank <= 1) & (n == 0), f32(0.0), f32(1.0))
        out_ref[0, rows, :] = head
        out_ref[1, rows, :] = rest[:, :BLOCK] * keep_second
        out_ref[2, rows, :] = (s2_ref[rows, :] + rest[:, BLOCK:]) * keep_schur
        for copy in copies(n):
            copy.start()
        return carry

    lax.fori_loop(0, ROW_STEPS, out_step, 0)
    for n in range(ROW_STEPS):
        for copy in copies(n):
            copy.wait()


def panel_chain(rank, mine, other, inv_length, features):
    vmem = pl.BlockSpec(memory_space=pltpu.VMEM)
    anywhere = pl.BlockSpec(memory_space=pl.ANY)
    return pl.pallas_call(
        chain_kernel,
        name="panel_chain",
        in_specs=[pl.BlockSpec(memory_space=pltpu.SMEM)] + [vmem] * 3 + [anywhere],
        out_specs=(anywhere, anywhere),
        out_shape=(
            jax.ShapeDtypeStruct((2, ROWS_DEV, BLOCK), f32),
            jax.ShapeDtypeStruct((ROWS_DEV, BLOCK), f32),
        ),
        scratch_shapes=[
            pltpu.VMEM((CHAIN, COLUMNS), f32),
            pltpu.VMEM((16, BLOCK), f32),
            pltpu.VMEM((BLOCK, BLOCK), i32),
            pltpu.VMEM((BLOCK, BLOCK), f32),
            pltpu.VMEM((40, BLOCK), i32),
            pltpu.VMEM((40, BLOCK), f32),
            pltpu.VMEM((PANEL, COLUMNS), bf16),
            pltpu.VMEM((8, COLUMNS), f32),
            pltpu.VMEM((COLUMNS, BLOCK), f32),
            pltpu.VMEM((BLOCK, COLUMNS), f32),
            pltpu.VMEM((BLOCK, BLOCK), f32),
            pltpu.VMEM((BLOCK, BLOCK), f32),
            pltpu.VMEM((CHAIN, COLUMNS), bf16),
            pltpu.VMEM((CHAIN, COLUMNS), bf16),
            pltpu.VMEM((CHAIN, CHAIN), bf16),
            pltpu.VMEM((CHAIN, CHAIN), bf16),
            pltpu.VMEM((ROWS_DEV, CHAIN), bf16),
            pltpu.VMEM((ROWS_DEV, CHAIN), bf16),
            pltpu.VMEM((ROWS_DEV, BLOCK), f32),
            pltpu.VMEM((CHAIN, 3 * BLOCK), bf16),
            pltpu.VMEM((CHAIN, 3 * BLOCK), bf16),
            pltpu.VMEM((3, ROWS_DEV, BLOCK), f32),
            pltpu.VMEM((ROWS_DEV, BLOCK), f32),
            pltpu.SemaphoreType.DMA((ROW_STEPS, 3)),
            pltpu.SemaphoreType.DMA,
        ],
        compiler_params=pltpu.CompilerParams(vmem_limit_bytes=VMEM_BYTES),
        cost_estimate=pl.CostEstimate(
            flops=6 * ROWS_DEV * COLUMNS * CHAIN, bytes_accessed=12 * 1024 * 1024, transcendentals=ROWS_DEV * COLUMNS
        ),
    )(rank, mine, other, inv_length, features)


def row_index(z, y, core):
    return (z % 4) * 8 + (y % 4) * 2 + core


def share_panels(features, nugget, tables):
    row = lax.axis_index("row")
    col = lax.axis_index("col")
    z, y = row // 8, (row // 2) % 4
    quarter = lax.dynamic_slice_in_dim(features, col * BLOCK, BLOCK, 0)
    extra = lax.dynamic_slice_in_dim(nugget.reshape(ROWS_DEV // BLOCK, BLOCK), col, 1, 0)
    mine = jnp.concatenate([quarter, jnp.broadcast_to(extra, (8, BLOCK))], 0)

    def send(value, pairs):
        return lax.ppermute(value, "row", pairs)

    along_z = [
        send(mine, [(row_index(0, *at), row_index(k, *at)) for at in ((0, 0), (0, 1), (1, 0))]) for k in (1, 2, 3)
    ]
    for k in (1, 2, 3):
        mine = jnp.where(z == k, along_z[k - 1], mine)
    along_y = [
        send(
            mine,
            [
                (row_index(k, at, half), row_index(k, at + s, half))
                for k in range(4)
                for at, half in ((0, 0), (0, 1), (1, 0))
            ],
        )
        for s in (1, 2, 3)
    ]
    first, third = mine, mine
    for s in (1, 2, 3):
        first = jnp.where(y == s, along_y[s - 1], first)
        third = jnp.where(y == (1 + s) % 4, along_y[s - 1], third)
    part = jnp.concatenate([first, tables], 0)
    parts = [part] + [lax.ppermute(part, "col", [((i + k) % 4, i) for i in range(4)]) for k in (1, 2, 3)]
    summed = (parts[0][QUARTER:] + parts[1][QUARTER:]) + (parts[2][QUARTER:] + parts[3][QUARTER:])
    held = jnp.concatenate([part[:QUARTER] for part in parts] + [summed, third], 0)
    return held, send(held, [(i, i ^ 1) for i in range(32)])


def per_device(features, inv_length, nugget, pairs, weights):
    rank = jnp.stack([lax.axis_index("row"), lax.axis_index("col")]).astype(i32)
    tables = pair_tables(rank, pairs, weights.reshape(1, CONFIGS))
    mine, other = share_panels(features, nugget, tables)
    return panel_chain(rank, mine, other, inv_length.reshape(1, BLOCK), features)


def solution(mesh):
    placed = (P("row", None), P(), P("row"), P(), P())
    return jax.shard_map(
        per_device,
        mesh=mesh,
        in_specs=placed,
        out_specs=(P(None, "row", "col"), P("row", "col")),
        check_vma=False,
    )
```
